256 devices in a mesh: tm: 128 (over x, y, z), head: 2 (over core).
Axes of the slice: x: 4, y: 4, z: 8, core: 2. Of those that a mesh axis runs over, the one named last changes fastest.
Arguments:
- video: bfloat16 [128, 128, 1024], P('tm'), may hold values from -12 to 12
- assign: int32 [128, 128], P('tm'), may hold values from 0 to 31, as said below
- w_query: bfloat16 [1024, 1024], replicated, may hold values from -0.1875 to 0.1875
- w_key: bfloat16 [1024, 1024], replicated, may hold values from -0.1875 to 0.1875
- w_value: bfloat16 [1024, 1024], replicated, may hold values from -0.1875 to 0.1875
- w_out: bfloat16 [1024, 1024], replicated, may hold values from -0.1875 to 0.1875
- cotangent: bfloat16 [128, 128, 1024], P('tm'), may hold values from -6 to 6
Outputs:
- attended: bfloat16 [128, 128, 1024], P('tm', None, 'head')
- video_grad: bfloat16 [128, 128, 1024], P('tm', None, 'head')
The draws below stay inside these ranges and needn't reach their ends.
Inputs may be any that keep to these rules, and one draw needn't show every extreme that they name: `assign`: every memory row of every segment is named by at least one token.
All inputs are finite; a program needn't handle non-finite values.
Results may differ from the reference program's by a relative error of at most 0.013.
The reference program's roundings to bfloat16 on the way (of `memory`, `weights`, `heads_out`, `grad_out`, `dscores` and `query_grad`) count: a program that leaves them out, or rounds other values in their place, can miss the bound.
Values may be sent and summed in bfloat16 or wider, within the bound.
No kernel may reach another device: no remote copies, remote signals or barrier semaphores. Data moves between devices by JAX's collectives and lax.ppermute only.
A program may use at most 128 MiB of HBM per device.

```python
import jax
import jax.numpy as jnp
from jax import lax

D = 1024
HEADS = 16
HEAD_DIM = 64
MEM = 32
TOK = 128
SEGS = 128


def draw_video(key, part):
    key = jax.random.fold_in(key, 11)
    key_base = jax.random.fold_in(key, 0)
    values = jax.random.normal(key_base, (SEGS, TOK, D), jnp.float32)
    return jnp.clip(values, -12.0, 12.0).astype(jnp.bfloat16)


def draw_assign(key, part):
    key = jax.random.fold_in(key, 23)
    key_base, key_perm = jax.random.split(key, 2)
    base = jax.random.randint(key_base, (SEGS, TOK), 0, MEM, jnp.int32)
    perm_keys = jax.random.split(key_perm, SEGS)
    orders = jax.vmap(lambda one_key: jax.random.permutation(one_key, TOK))(perm_keys)
    row_ids = jnp.arange(SEGS, dtype=jnp.int32)[:, None]
    labels = jnp.broadcast_to(jnp.arange(MEM, dtype=jnp.int32)[None, :], (SEGS, MEM))
    return base.at[row_ids, orders[:, :MEM]].set(labels)


def levels(rng, shape, cuts, smallest, largest):
    def one(axis_at, blocks):
        steps = jax.random.uniform(jax.random.fold_in(jax.random.fold_in(rng, 6), axis_at), (blocks,), jnp.float32, smallest / len(cuts), largest / len(cuts))
        return jnp.repeat(jnp.exp(steps), shape[axis_at] // blocks).reshape((-1,) + (1,) * (len(shape) - axis_at - 1))

    level = one(*cuts[0])
    for cut in cuts[1:]:
        level = level * one(*cut)
    return level


def scatter_about(key, extent, scale, limit, shards=(), kind=jnp.bfloat16):
    gain = levels(key, extent, shards, -0.22, 0.18) if shards else 1.0
    drawn = jax.random.normal(key, extent, jnp.float32) * scale * gain
    return jnp.minimum(jnp.maximum(drawn, -limit), limit).astype(kind)


def setup_inputs(seed: int = 0) -> dict:
    keys = jax.random.split(jax.random.key(seed), 8)
    video = draw_video(jax.random.fold_in(keys[7], 71), 0)
    assign = draw_assign(jax.random.fold_in(keys[7], 71), 0)
    w_query = scatter_about(keys[2], (D, D), D ** -0.5, 0.1875)
    w_key = scatter_about(keys[3], (D, D), D ** -0.5, 0.1875)
    w_value = scatter_about(keys[4], (D, D), D ** -0.5, 0.1875)
    w_out = scatter_about(keys[5], (D, D), D ** -0.5, 0.1875)
    cotangent = scatter_about(keys[6], (SEGS, TOK, D), 1.0, 6.0, ((0, 128),))
    return {"video": video, "assign": assign, "w_query": w_query, "w_key": w_key, "w_value": w_value, "w_out": w_out, "cotangent": cotangent}


def reference(video, assign, w_query, w_key, w_value, w_out, cotangent):
    score_scale = HEAD_DIM ** -0.5
    prior_rows = SEGS * MEM
    flat_video = video.reshape(SEGS * TOK, D)

    def project(weight):
        return jnp.dot(flat_video, weight, preferred_element_type=jnp.float32).astype(jnp.bfloat16).reshape(SEGS, TOK, D)

    query_rows = project(w_query)
    key_rows = project(w_key)
    value_rows = project(w_value)
    onehot = (assign[:, :, None] == jnp.arange(MEM, dtype=jnp.int32)[None, None, :]).astype(jnp.float32)
    counts = jnp.sum(onehot, axis=1)
    summed = jnp.einsum("stm,std->smd", onehot, video.astype(jnp.float32), precision=lax.Precision.HIGHEST)
    memory = (summed / counts[:, :, None]).astype(jnp.bfloat16).reshape(prior_rows, D)
    mem_keys = jnp.dot(memory, w_key, preferred_element_type=jnp.float32).astype(jnp.bfloat16)
    mem_values = jnp.dot(memory, w_value, preferred_element_type=jnp.float32).astype(jnp.bfloat16)
    key_index = jnp.arange(prior_rows + TOK, dtype=jnp.int32)

    def segment_step(accum, inputs):
        queries, own_keys, own_values, grad_in, segment = inputs
        visible = (key_index < segment * MEM) | (key_index >= prior_rows)
        all_keys = jnp.concatenate([mem_keys, own_keys], axis=0).astype(jnp.float32).reshape(-1, HEADS, HEAD_DIM)
        all_values = jnp.concatenate([mem_values, own_values], axis=0).astype(jnp.float32).reshape(-1, HEADS, HEAD_DIM)
        query_heads = queries.astype(jnp.float32).reshape(TOK, HEADS, HEAD_DIM)
        scores = jnp.einsum("thd,jhd->htj", query_heads, all_keys) * score_scale
        row_max = jnp.max(jnp.where(visible[None, None, :], scores, -jnp.inf), axis=2, keepdims=True)
        raised = jnp.where(visible[None, None, :], jnp.exp(scores - row_max), 0.0)
        probs = raised / jnp.sum(raised, axis=2, keepdims=True)
        weights = probs.astype(jnp.bfloat16)
        heads_out = jnp.einsum("htj,jhd->thd", weights.astype(jnp.float32), all_values).astype(jnp.bfloat16)
        heads_flat = heads_out.reshape(TOK, D)
        attended = jnp.dot(heads_flat, w_out, preferred_element_type=jnp.float32).astype(jnp.bfloat16)
        grad_out = jnp.dot(grad_in, w_out.T, preferred_element_type=jnp.float32).astype(jnp.bfloat16)
        grad_heads = grad_out.astype(jnp.float32).reshape(TOK, HEADS, HEAD_DIM)
        row_delta = jnp.einsum("thd,thd->ht", grad_heads, heads_out.astype(jnp.float32))
        dprobs = jnp.einsum("thd,jhd->htj", grad_heads, all_values)
        dscores = (probs * (dprobs - row_delta[:, :, None])).astype(jnp.bfloat16).astype(jnp.float32)
        query_grad = (jnp.einsum("htj,jhd->thd", dscores, all_keys) * score_scale).astype(jnp.bfloat16).reshape(TOK, D)
        key_grads = jnp.einsum("htj,thd->jhd", dscores, query_heads).reshape(-1, D) * score_scale
        value_grads = jnp.einsum("htj,thd->jhd", weights.astype(jnp.float32), grad_heads).reshape(-1, D)
        key_grad = key_grads[prior_rows:].astype(jnp.bfloat16)
        value_grad = value_grads[prior_rows:].astype(jnp.bfloat16)
        accum = accum + jnp.concatenate([key_grads[:prior_rows], value_grads[:prior_rows]], axis=1)
        local_grad = jnp.dot(query_grad, w_query.T, preferred_element_type=jnp.float32)
        local_grad = local_grad + jnp.dot(key_grad, w_key.T, preferred_element_type=jnp.float32)
        local_grad = local_grad + jnp.dot(value_grad, w_value.T, preferred_element_type=jnp.float32)
        return accum, (attended, local_grad)

    start_accum = jnp.zeros((prior_rows, 2 * D), jnp.float32)
    accum, (attended, local_grads) = lax.scan(
        segment_step, start_accum,
        (query_rows, key_rows, value_rows, cotangent, jnp.arange(SEGS, dtype=jnp.int32)))
    mem_key_grad = accum[:, :D].astype(jnp.bfloat16)
    mem_value_grad = accum[:, D:].astype(jnp.bfloat16)
    memory_grad = jnp.dot(mem_key_grad, w_key.T, preferred_element_type=jnp.float32)
    memory_grad = memory_grad + jnp.dot(mem_value_grad, w_value.T, preferred_element_type=jnp.float32)
    mem_term = memory_grad.reshape(SEGS, MEM, D) / counts[:, :, None]
    spread = jnp.einsum("stm,smd->std", onehot, mem_term, precision=lax.Precision.HIGHEST)
    video_grad = (local_grads + spread).astype(jnp.bfloat16)
    return attended, video_grad
```

```python
import functools

import jax
import jax.numpy as jnp
from jax import lax
from jax.experimental import pallas as pl
from jax.experimental.pallas import tpu as pltpu
from jax.sharding import PartitionSpec as P

HEAD_DIM = 64
MEM = 32
TOK = 128
D = 1024
HALF = 512
LOCAL_HEADS = 8
SPLITS = 16
CHIPS = 128
QROWS = TOK // SPLITS
ROWS = MEM + 2 * QROWS
LANES = 2 * HEAD_DIM
KEYS = CHIPS * MEM
BLOCK_SEGS = 16
QBLOCK = BLOCK_SEGS * QROWS
KBLOCK = BLOCK_SEGS * MEM
NBLOCKS = CHIPS // BLOCK_SEGS
SCALE = 0.125
MASKED = -3e38
VMEM_BYTES = 40 * 1024 * 1024
f32 = jnp.float32
bf16 = jnp.bfloat16


def dot(a, b):
    return jnp.dot(a, b, preferred_element_type=f32)


def dot_nt(a, b):
    return lax.dot_general(a, b, (((1,), (1,)), ((), ())), preferred_element_type=f32)


def dot_tn(a, b):
    return lax.dot_general(a, b, (((0,), (0,)), ((), ())), preferred_element_type=f32)


def three_parts(x):
    high = x.astype(bf16).astype(f32)
    rest = x - high
    middle = rest.astype(bf16).astype(f32)
    low = (rest - middle).astype(bf16).astype(f32)
    return high, middle, low


def low_lanes(shape):
    return lax.broadcasted_iota(jnp.int32, shape, 1) < HEAD_DIM


def split_pair(pair):
    low = low_lanes(pair.shape)
    zero = jnp.zeros_like(pair)
    return jnp.concatenate([jnp.where(low, pair, zero), jnp.where(low, zero, pair)], axis=0)


def head_cols(matrix, head):
    return matrix[:, head * HEAD_DIM : (head + 1) * HEAD_DIM]


def onehot_rows(assign_row):
    rows = lax.broadcasted_iota(jnp.int32, (MEM, TOK), 0)
    return (rows == assign_row).astype(f32)


def pre_kernel(tok_ref, asg_ref, cot_ref, wq_hbm, wk_hbm, wv_hbm, wo_hbm, msg_ref, qd_ref, kv_ref, wq, wk, wv, wo, sems):
    offset = pl.multiple_of(lax.axis_index("head") * HALF, HALF)
    copies = [
        pltpu.make_async_copy(wk_hbm.at[:, pl.ds(offset, HALF)], wk, sems.at[0]),
        pltpu.make_async_copy(wv_hbm.at[:, pl.ds(offset, HALF)], wv, sems.at[1]),
        pltpu.make_async_copy(wq_hbm.at[:, pl.ds(offset, HALF)], wq, sems.at[2]),
        pltpu.make_async_copy(wo_hbm.at[pl.ds(offset, HALF), :], wo, sems.at[3]),
    ]
    for copy in copies:
        copy.start()
    tokens = tok_ref[...]
    onehot = onehot_rows(asg_ref[...])
    counts = jnp.sum(onehot, axis=1, keepdims=True)
    memory = (dot(onehot.astype(bf16), tokens) / counts).astype(bf16)
    rows = jnp.concatenate([memory, tokens], axis=0)
    copies[0].wait()
    keys = dot(rows, wk[...]).astype(bf16)
    copies[1].wait()
    values = dot(rows, wv[...]).astype(bf16)
    copies[2].wait()
    queries = (dot(tokens, wq[...]).astype(bf16).astype(f32) * SCALE).astype(bf16)
    copies[3].wait()
    grad_out = dot_nt(cot_ref[...], wo[...]).astype(bf16)
    lane = lax.broadcasted_iota(jnp.int32, (TOK, LANES), 1)
    for head in range(LOCAL_HEADS):
        pair = jnp.concatenate([head_cols(keys, head), head_cols(values, head)], axis=1)
        query_pair = jnp.concatenate([head_cols(queries, head), head_cols(grad_out, head)], axis=1)
        own = pair[MEM:]
        kv_ref[head] = own
        qd_ref[head] = query_pair
        masked = jnp.where(low_lanes(query_pair.shape), query_pair, jnp.zeros_like(query_pair))
        scores = dot_nt(masked, own)
        row_max = jnp.max(scores, axis=1, keepdims=True)
        raised = jnp.exp(scores - row_max)
        row_sum = jnp.sum(raised, axis=1, keepdims=True)
        out = dot((raised / row_sum).astype(bf16), own)
        side = out
        for at, part in enumerate(three_parts(row_max) + three_parts(row_sum)):
            side = jnp.where(lane == at, part, side)
        both = jnp.concatenate(
            [query_pair.astype(f32).reshape(SPLITS, QROWS, LANES), side.reshape(SPLITS, QROWS, LANES)], axis=1
        ).astype(bf16)
        msg_ref[:, head, :MEM, :] = jnp.broadcast_to(pair[:MEM][None], (SPLITS, MEM, LANES))
        msg_ref[:, head, MEM:, :] = both


def attend_kernel(msg_ref, out_ref, kvt, scores, dprobs, pairs, accum):
    def block(j):
        return pl.ds(pl.multiple_of(j * KBLOCK, KBLOCK), KBLOCK)

    def kv_block(j):
        return msg_ref[pl.ds(j * BLOCK_SEGS, BLOCK_SEGS), :MEM, :].reshape(KBLOCK, LANES)

    eye = (
        lax.broadcasted_iota(jnp.int32, (LANES, LANES), 0) == lax.broadcasted_iota(jnp.int32, (LANES, LANES), 1)
    ).astype(bf16)

    for j in range(NBLOCKS):
        kvt[:, j * KBLOCK : (j + 1) * KBLOCK] = dot_nt(eye, kv_block(j)).astype(bf16)
        accum[j * KBLOCK : (j + 1) * KBLOCK, :] = jnp.zeros((KBLOCK, LANES), f32)

    visible = lax.broadcasted_iota(jnp.int32, (KBLOCK, QBLOCK), 0) // MEM < (
        lax.broadcasted_iota(jnp.int32, (KBLOCK, QBLOCK), 1) // QROWS
    )

    def fold(op, x):
        return op(x.reshape(KBLOCK // 8, 8, QBLOCK), axis=0)

    def query_block(i, carry):
        rows = msg_ref[pl.ds(i * BLOCK_SEGS, BLOCK_SEGS), MEM:, :].astype(f32)
        query_pair = rows[:, :QROWS].reshape(QBLOCK, LANES)
        side = rows[:, QROWS:].reshape(QBLOCK, LANES).T
        own_out = side[HEAD_DIM:]
        own_max = side[0:1] + side[1:2] + side[2:3]
        own_sum = side[3:4] + side[4:5] + side[5:6]
        grad_t = query_pair.T[HEAD_DIM:]
        pair_rows = split_pair(query_pair).astype(bf16)

        def first(j, top, mask):
            both = dot_nt(kv_block(j), pair_rows)
            score = both[:, :QBLOCK]
            if mask:
                score = jnp.where(visible, score, MASKED)
            scores[block(j), :] = score
            dprobs[block(j), :] = both[:, QBLOCK:]
            return jnp.maximum(top, fold(jnp.max, score))

        top = jnp.broadcast_to(own_max, (8, QBLOCK))
        top = lax.fori_loop(0, i, lambda j, t: first(j, t, False), top)
        top = first(i, top, True)
        row_max = jnp.max(top, axis=0, keepdims=True)

        def second(j, total):
            raised = jnp.exp(scores[block(j), :] - row_max)
            scores[block(j), :] = raised
            return total + fold(jnp.sum, raised)

        total = lax.fori_loop(0, i + 1, second, jnp.zeros((8, QBLOCK), f32))
        own_share = own_sum * jnp.exp(own_max - row_max)
        row_sum = own_share + jnp.sum(total, axis=0, keepdims=True)
        inverse = 1.0 / row_sum

        def third(j, out):
            probs = scores[block(j), :] * inverse
            scores[block(j), :] = probs
            weights = probs.astype(bf16)
            pairs[block(j), QBLOCK:] = weights
            return out + dot(kvt[:, block(j)], weights)

        out = lax.fori_loop(0, i + 1, third, jnp.zeros((LANES, QBLOCK), f32))
        heads_out = (own_out * (own_share * inverse) + out[HEAD_DIM:]).astype(bf16).astype(f32)
        delta = jnp.sum(grad_t * heads_out, axis=0, keepdims=True)

        def fourth(j, grad):
            dscores = (scores[block(j), :] * (dprobs[block(j), :] - delta)).astype(bf16)
            pairs[block(j), :QBLOCK] = dscores
            accum[block(j), :] += dot(pairs[block(j), :], pair_rows)
            return grad + dot(kvt[:, block(j)], dscores)

        query_grad = lax.fori_loop(0, i + 1, fourth, jnp.zeros((LANES, QBLOCK), f32))[:HEAD_DIM]
        grad_high = query_grad.astype(bf16).astype(f32)
        main = jnp.concatenate([grad_high, heads_out], axis=0).T
        row_at = lax.broadcasted_iota(jnp.int32, (HEAD_DIM, QBLOCK), 0)
        stats = jnp.zeros((HEAD_DIM, QBLOCK), f32)
        for at, part in enumerate(three_parts(row_max) + three_parts(row_sum)):
            stats = jnp.where(row_at == at, part, stats)
        extra = jnp.concatenate([query_grad - grad_high, stats], axis=0).T
        out_ref[pl.ds(i * BLOCK_SEGS, BLOCK_SEGS), MEM:, :] = jnp.concatenate(
            [main.reshape(BLOCK_SEGS, QROWS, LANES), extra.reshape(BLOCK_SEGS, QROWS, LANES)], axis=1
        ).astype(bf16)
        return carry

    lax.fori_loop(0, NBLOCKS, query_block, 0)
    for j in range(NBLOCKS):
        out_ref[j * BLOCK_SEGS : (j + 1) * BLOCK_SEGS, :MEM, :] = (
            accum[j * KBLOCK : (j + 1) * KBLOCK, :].astype(bf16).reshape(BLOCK_SEGS, MEM, LANES)
        )


def post_kernel(msg_ref, asg_ref, qd_ref, kv_ref, wq_hbm, wk_hbm, wv_hbm, wo_hbm, mine_ref, other_ref, wq, wk, wv, wo, sems):
    half = lax.axis_index("head")
    offset = pl.multiple_of(half * HALF, HALF)
    away = pl.multiple_of((1 - half) * HALF, HALF)
    copies = [
        pltpu.make_async_copy(wo_hbm.at[pl.ds(offset, HALF), :], wo, sems.at[0]),
        pltpu.make_async_copy(wq_hbm.at[:, pl.ds(offset, HALF)], wq, sems.at[1]),
        pltpu.make_async_copy(wk_hbm.at[:, pl.ds(offset, HALF)], wk, sems.at[2]),
        pltpu.make_async_copy(wv_hbm.at[:, pl.ds(offset, HALF)], wv, sems.at[3]),
    ]
    for copy in copies:
        copy.start()
    onehot = onehot_rows(asg_ref[...])
    counts = jnp.sum(onehot, axis=1, keepdims=True)
    heads_out, query_grads, key_grads, value_grads = [], [], [], []
    for head in range(LOCAL_HEADS):
        mem_pair = jnp.sum(msg_ref[:, head, :MEM, :].astype(f32), axis=0)
        rows = msg_ref[:, head, MEM:, :].astype(f32)
        main = rows[:, :QROWS].reshape(TOK, LANES)
        extra = rows[:, QROWS:].reshape(TOK, LANES)
        at = HEAD_DIM
        row_max = extra[:, at : at + 1] + extra[:, at + 1 : at + 2] + extra[:, at + 2 : at + 3]
        row_sum = extra[:, at + 3 : at + 4] + extra[:, at + 4 : at + 5] + extra[:, at + 5 : at + 6]
        query_pair = qd_ref[head]
        own = kv_ref[head]
        pair_rows = split_pair(query_pair)
        both = dot_nt(pair_rows, own)
        probs = jnp.exp(both[:TOK] - row_max) / row_sum
        weights = probs.astype(bf16)
        products = query_pair.astype(f32) * main
        delta = jnp.sum(jnp.where(low_lanes(products.shape), 0.0, products), axis=1, keepdims=True)
        dscores = (probs * (both[TOK:] - delta)).astype(bf16)
        query_grad = (main + extra + dot(dscores, own)) * SCALE
        own_pair = dot_tn(jnp.concatenate([dscores, weights], axis=0), pair_rows)
        grads = jnp.concatenate([own_pair, mem_pair], axis=0)
        heads_out.append(main[:, HEAD_DIM:])
        query_grads.append(query_grad[:, :HEAD_DIM])
        key_grads.append(grads[:, :HEAD_DIM])
        value_grads.append(grads[:, HEAD_DIM:])

    def merge(parts):
        return jnp.concatenate(parts, axis=1).astype(bf16)

    heads_out = merge(heads_out)
    query_grads = merge(query_grads)
    key_grads = merge(key_grads)
    value_grads = merge(value_grads)
    onehot = onehot.astype(bf16)
    for copy in copies:
        copy.wait()
    for ref, start in ((mine_ref, offset), (other_ref, away)):
        rows = pl.ds(start, HALF)
        ref[0] = dot(heads_out, wo[:, rows])
        total = dot_nt(key_grads, wk[rows, :]) + dot_nt(value_grads, wv[rows, :])
        high, middle, low = three_parts(total[TOK:] / counts)
        spread = dot_tn(onehot, high.astype(bf16)) + dot_tn(onehot, middle.astype(bf16)) + dot_tn(onehot, low.astype(bf16))
        ref[1] = total[:TOK] + dot_nt(query_grads, wq[rows, :]) + spread


def params():
    return pltpu.CompilerParams(vmem_limit_bytes=VMEM_BYTES)


def vmem():
    return pl.BlockSpec(memory_space=pltpu.VMEM)


def hbm():
    return pl.BlockSpec(memory_space=pl.ANY)


def weight_scratch():
    return [pltpu.VMEM((D, HALF), bf16)] * 3 + [pltpu.VMEM((HALF, D), bf16), pltpu.SemaphoreType.DMA((4,))]


def shards(video, assign, w_query, w_key, w_value, w_out, cotangent):
    pair_shape = jax.ShapeDtypeStruct((LOCAL_HEADS, TOK, LANES), bf16)
    message_shape = jax.ShapeDtypeStruct((SPLITS, LOCAL_HEADS, ROWS, LANES), bf16)
    message, query_pairs, own_pairs = pl.pallas_call(
        pre_kernel,
        out_shape=(message_shape, pair_shape, pair_shape),
        in_specs=[vmem()] * 3 + [hbm()] * 4,
        out_specs=(vmem(), vmem(), vmem()),
        scratch_shapes=weight_scratch(),
        compiler_params=params(),
        name="project",
    )(video[0], assign, cotangent[0], w_query, w_key, w_value, w_out)

    received = lax.all_to_all(message.reshape(CHIPS, ROWS, LANES), "tm", 0, 0, tiled=True)
    answer = pl.pallas_call(
        attend_kernel,
        out_shape=jax.ShapeDtypeStruct((CHIPS, ROWS, LANES), bf16),
        in_specs=[vmem()],
        out_specs=vmem(),
        scratch_shapes=[
            pltpu.VMEM((LANES, KEYS), bf16),
            pltpu.VMEM((KEYS, QBLOCK), f32),
            pltpu.VMEM((KEYS, QBLOCK), f32),
            pltpu.VMEM((KEYS, 2 * QBLOCK), bf16),
            pltpu.VMEM((KEYS, LANES), f32),
        ],
        compiler_params=params(),
        name="attend",
    )(received)
    returned = lax.all_to_all(answer, "tm", 0, 0, tiled=True).reshape(message_shape.shape)

    half_shape = jax.ShapeDtypeStruct((2, TOK, HALF), f32)
    mine, other = pl.pallas_call(
        post_kernel,
        out_shape=(half_shape, half_shape),
        in_specs=[vmem()] * 4 + [hbm()] * 4,
        out_specs=(vmem(), vmem()),
        scratch_shapes=weight_scratch(),
        compiler_params=params(),
        name="gradients",
    )(returned, assign, query_pairs, own_pairs, w_query, w_key, w_value, w_out)
    total = mine + lax.ppermute(other, "head", [(0, 1), (1, 0)])
    total = total.astype(bf16)
    return (total[0][None], total[1][None])


def solution(mesh):
    placed = (P("tm", None, None), P("tm", None), P(), P(), P(), P(), P("tm", None, None))
    return jax.shard_map(
        shards,
        mesh=mesh,
        in_specs=placed,
        out_specs=(P("tm", None, "head"), P("tm", None, "head")),
        check_vma=False,
    )
```

```python
import jax
import jax.numpy as jnp
from jax import lax
from jax.experimental import pallas as pl
from jax.experimental.pallas import tpu as pltpu
from jax.sharding import PartitionSpec as P

HEAD_DIM = 64
MEM = 32
TOK = 128
D = 1024
HALF = 512
LOCAL_HEADS = 8
SPLITS = 16
CHIPS = 128
QROWS = TOK // SPLITS
ROWS = MEM + 2 * QROWS
LANES = 2 * HEAD_DIM
KEYS = CHIPS * MEM
BLOCK_SEGS = 16
QBLOCK = BLOCK_SEGS * QROWS
KBLOCK = BLOCK_SEGS * MEM
NBLOCKS = CHIPS // BLOCK_SEGS
SCALE = 0.125
MASKED = -3e38
FIRST_VMEM = 60 * 1024 * 1024
MIDDLE_VMEM = 32 * 1024 * 1024
LAST_VMEM = 32 * 1024 * 1024
f32 = jnp.float32
bf16 = jnp.bfloat16


def dot(a, b):
    return jnp.dot(a, b, preferred_element_type=f32)


def dot_nt(a, b):
    return lax.dot_general(a, b, (((1,), (1,)), ((), ())), preferred_element_type=f32)


def dot_tn(a, b):
    return lax.dot_general(a, b, (((0,), (0,)), ((), ())), preferred_element_type=f32)


def three_parts(x):
    high = x.astype(bf16).astype(f32)
    rest = x - high
    middle = rest.astype(bf16).astype(f32)
    low = (rest - middle).astype(bf16).astype(f32)
    return high, middle, low


def low_lanes(shape):
    return lax.broadcasted_iota(jnp.int32, shape, 1) < HEAD_DIM


def split_pair(pair):
    low = low_lanes(pair.shape)
    zero = jnp.zeros_like(pair)
    return jnp.concatenate([jnp.where(low, pair, zero), jnp.where(low, zero, pair)], axis=0)


def head_cols(matrix, head):
    return matrix[:, head * HEAD_DIM : (head + 1) * HEAD_DIM]


def onehot_rows(assign_row):
    rows = lax.broadcasted_iota(jnp.int32, (MEM, TOK), 0)
    return (rows == assign_row).astype(f32)


def pre_kernel(
    tok_hbm, asg_hbm, cot_hbm, wq_hbm, wk_hbm, wv_hbm, wo_hbm, msg_hbm, qd_ref, kv_ref,
    tok_ref, asg_ref, cot_ref, wq, wk, wv, wo, msg_ref, sems, out_sems,
):
    offset = pl.multiple_of(lax.axis_index("head") * HALF, HALF)
    moves = [
        (asg_hbm, asg_ref),
        (tok_hbm, tok_ref),
        (wk_hbm.at[:, pl.ds(offset, HALF)], wk),
        (wv_hbm.at[:, pl.ds(offset, HALF)], wv),
        (wq_hbm.at[:, pl.ds(offset, HALF)], wq),
        (cot_hbm, cot_ref),
        (wo_hbm.at[pl.ds(offset, HALF), :], wo),
    ]
    copies = [pltpu.make_async_copy(source, target, sems.at[at]) for at, (source, target) in enumerate(moves)]
    for copy in copies:
        copy.start()
    copies[0].wait()
    onehot = onehot_rows(asg_ref[...])
    counts = jnp.sum(onehot, axis=1, keepdims=True)
    copies[1].wait()
    tokens = tok_ref[...]
    memory = (dot(onehot.astype(bf16), tokens) / counts).astype(bf16)
    rows = jnp.concatenate([memory, tokens], axis=0)
    copies[2].wait()
    keys = dot(rows, wk[...]).astype(bf16)
    copies[3].wait()
    values = dot(rows, wv[...]).astype(bf16)
    copies[4].wait()
    queries = (dot(tokens, wq[...]).astype(bf16).astype(f32) * SCALE).astype(bf16)
    copies[5].wait()
    copies[6].wait()
    grad_out = dot_nt(cot_ref[...], wo[...]).astype(bf16)
    lane = lax.broadcasted_iota(jnp.int32, (TOK, LANES), 1)
    sends = []
    for head in range(LOCAL_HEADS):
        pair = jnp.concatenate([head_cols(keys, head), head_cols(values, head)], axis=1)
        query_pair = jnp.concatenate([head_cols(queries, head), head_cols(grad_out, head)], axis=1)
        own = pair[MEM:]
        kv_ref[head] = own
        qd_ref[head] = query_pair
        masked = jnp.where(low_lanes(query_pair.shape), query_pair, jnp.zeros_like(query_pair))
        scores = dot_nt(masked, own)
        row_max = jnp.max(scores, axis=1, keepdims=True)
        raised = jnp.exp(scores - row_max)
        row_sum = jnp.sum(raised, axis=1, keepdims=True)
        out = dot((raised / row_sum).astype(bf16), own)
        side = out
        for at, part in enumerate(three_parts(row_max) + three_parts(row_sum)):
            side = jnp.where(lane == at, part, side)
        both = jnp.concatenate(
            [query_pair.astype(f32).reshape(SPLITS, QROWS, LANES), side.reshape(SPLITS, QROWS, LANES)], axis=1
        ).astype(bf16)
        msg_ref[:, head, :MEM, :] = jnp.broadcast_to(pair[:MEM][None], (SPLITS, MEM, LANES))
        msg_ref[:, head, MEM:, :] = both
        sends.append(pltpu.make_async_copy(msg_ref.at[:, head], msg_hbm.at[:, head], out_sems.at[head]))
        sends[-1].start()
    for send in sends:
        send.wait()


def attend_kernel(msg_hbm, out_hbm, msg_ref, out_ref, kvt, scores, dprobs, accum, in_sems, out_sem):
    def segs(j):
        return slice(j * BLOCK_SEGS, (j + 1) * BLOCK_SEGS)

    def block(j):
        return slice(j * KBLOCK, (j + 1) * KBLOCK)

    def kv_block(j):
        return msg_ref[segs(j), :MEM, :].reshape(KBLOCK, LANES)

    copies = [pltpu.make_async_copy(msg_hbm.at[segs(j)], msg_ref.at[segs(j)], in_sems.at[j]) for j in range(NBLOCKS)]
    for copy in copies:
        copy.start()
    eye = (
        lax.broadcasted_iota(jnp.int32, (LANES, LANES), 0) == lax.broadcasted_iota(jnp.int32, (LANES, LANES), 1)
    ).astype(bf16)
    visible = lax.broadcasted_iota(jnp.int32, (KBLOCK, QBLOCK), 0) // MEM < (
        lax.broadcasted_iota(jnp.int32, (KBLOCK, QBLOCK), 1) // QROWS
    )

    def fold(op, x):
        return op(x.reshape(KBLOCK // 8, 8, QBLOCK), axis=0)

    for i in range(NBLOCKS):
        buf = i % 2
        copies[i].wait()
        kvt[:, block(i)] = dot_nt(eye, kv_block(i)).astype(bf16)
        rows = msg_ref[segs(i), MEM:, :].astype(f32)
        query_pair = rows[:, :QROWS].reshape(QBLOCK, LANES)
        side = rows[:, QROWS:].reshape(QBLOCK, LANES).T
        own_out = side[HEAD_DIM:]
        own_max = side[0:1] + side[1:2] + side[2:3]
        own_sum = side[3:4] + side[4:5] + side[5:6]
        grad_t = query_pair.T[HEAD_DIM:]
        pair_rows = split_pair(query_pair).astype(bf16)

        top = jnp.broadcast_to(own_max, (8, QBLOCK))
        for j in range(i + 1):
            both = dot_nt(kv_block(j), pair_rows)
            score = both[:, :QBLOCK]
            if j == i:
                score = jnp.where(visible, score, MASKED)
            scores[buf, block(j), :] = score
            dprobs[buf, block(j), :] = both[:, QBLOCK:]
            top = jnp.maximum(top, fold(jnp.max, score))
        row_max = jnp.max(top, axis=0, keepdims=True)

        total = jnp.zeros((8, QBLOCK), f32)
        out = jnp.zeros((LANES, QBLOCK), f32)
        for j in range(i + 1):
            raised = jnp.exp(scores[buf, block(j), :] - row_max)
            scores[buf, block(j), :] = raised
            total = total + fold(jnp.sum, raised)
            out = out + dot(kvt[:, block(j)], raised.astype(bf16))
        own_share = own_sum * jnp.exp(own_max - row_max)
        row_sum = own_share + jnp.sum(total, axis=0, keepdims=True)
        inverse = 1.0 / row_sum
        heads_out = ((own_out * own_share + out[HEAD_DIM:]) * inverse).astype(bf16).astype(f32)
        delta = jnp.sum(grad_t * heads_out, axis=0, keepdims=True)

        grad = jnp.zeros((LANES, QBLOCK), f32)
        for j in range(i + 1):
            probs = scores[buf, block(j), :] * inverse
            dscores = (probs * (dprobs[buf, block(j), :] - delta)).astype(bf16)
            both = jnp.concatenate([dscores, probs.astype(bf16)], axis=1)
            term = dot(both, pair_rows)
            if j == i:
                accum[block(j), :] = term
            else:
                accum[block(j), :] += term
            grad = grad + dot(kvt[:, block(j)], dscores)
        query_grad = grad[:HEAD_DIM]
        grad_high = query_grad.astype(bf16).astype(f32)
        main = jnp.concatenate([grad_high, heads_out], axis=0).T
        row_at = lax.broadcasted_iota(jnp.int32, (HEAD_DIM, QBLOCK), 0)
        stats = jnp.zeros((HEAD_DIM, QBLOCK), f32)
        for at, part in enumerate(three_parts(row_max) + three_parts(row_sum)):
            stats = jnp.where(row_at == at, part, stats)
        extra = jnp.concatenate([query_grad - grad_high, stats], axis=0).T
        out_ref[segs(i), MEM:, :] = jnp.concatenate(
            [main.reshape(BLOCK_SEGS, QROWS, LANES), extra.reshape(BLOCK_SEGS, QROWS, LANES)], axis=1
        ).astype(bf16)

    for j in range(NBLOCKS):
        out_ref[segs(j), :MEM, :] = accum[block(j), :].astype(bf16).reshape(BLOCK_SEGS, MEM, LANES)
    copy = pltpu.make_async_copy(out_ref, out_hbm, out_sem)
    copy.start()
    copy.wait()


def post_kernel(
    msg_hbm, asg_ref, qd_ref, kv_ref, wq_hbm, wk_hbm, wv_hbm, wo_hbm, mine_ref, other_ref,
    wq, wk, wv, wo, msg_ref, sems, in_sems,
):
    half = lax.axis_index("head")
    offset = pl.multiple_of(half * HALF, HALF)
    away = pl.multiple_of((1 - half) * HALF, HALF)
    copies = [
        pltpu.make_async_copy(wo_hbm.at[pl.ds(offset, HALF), :], wo, sems.at[0]),
        pltpu.make_async_copy(wq_hbm.at[:, pl.ds(offset, HALF)], wq, sems.at[1]),
        pltpu.make_async_copy(wk_hbm.at[:, pl.ds(offset, HALF)], wk, sems.at[2]),
        pltpu.make_async_copy(wv_hbm.at[:, pl.ds(offset, HALF)], wv, sems.at[3]),
    ]
    parts = [
        pltpu.make_async_copy(msg_hbm.at[:, head], msg_ref.at[:, head], in_sems.at[head]) for head in range(LOCAL_HEADS)
    ]
    for copy in parts + copies:
        copy.start()
    onehot = onehot_rows(asg_ref[...])
    counts = jnp.sum(onehot, axis=1, keepdims=True)
    heads_out, query_grads, key_grads, value_grads = [], [], [], []
    for head in range(LOCAL_HEADS):
        parts[head].wait()
        mem_pair = jnp.sum(msg_ref[:, head, :MEM, :].astype(f32), axis=0)
        rows = msg_ref[:, head, MEM:, :].astype(f32)
        main = rows[:, :QROWS].reshape(TOK, LANES)
        extra = rows[:, QROWS:].reshape(TOK, LANES)
        at = HEAD_DIM
        row_max = extra[:, at : at + 1] + extra[:, at + 1 : at + 2] + extra[:, at + 2 : at + 3]
        row_sum = extra[:, at + 3 : at + 4] + extra[:, at + 4 : at + 5] + extra[:, at + 5 : at + 6]
        query_pair = qd_ref[head]
        own = kv_ref[head]
        pair_rows = split_pair(query_pair)
        both = dot_nt(pair_rows, own)
        probs = jnp.exp(both[:TOK] - row_max) / row_sum
        weights = probs.astype(bf16)
        products = query_pair.astype(f32) * main
        delta = jnp.sum(jnp.where(low_lanes(products.shape), 0.0, products), axis=1, keepdims=True)
        dscores = (probs * (both[TOK:] - delta)).astype(bf16)
        query_grad = (main + extra + dot(dscores, own)) * SCALE
        own_pair = dot_tn(jnp.concatenate([dscores, weights], axis=0), pair_rows)
        grads = jnp.concatenate([own_pair, mem_pair], axis=0)
        heads_out.append(main[:, HEAD_DIM:])
        query_grads.append(query_grad[:, :HEAD_DIM])
        key_grads.append(grads[:, :HEAD_DIM])
        value_grads.append(grads[:, HEAD_DIM:])

    def merge(parts):
        return jnp.concatenate(parts, axis=1).astype(bf16)

    heads_out = merge(heads_out)
    query_grads = merge(query_grads)
    key_grads = merge(key_grads)
    value_grads = merge(value_grads)
    onehot = onehot.astype(bf16)
    for copy in copies:
        copy.wait()
    for ref, start in ((mine_ref, offset), (other_ref, away)):
        rows = pl.ds(start, HALF)
        ref[0] = dot(heads_out, wo[:, rows])
        total = dot_nt(key_grads, wk[rows, :]) + dot_nt(value_grads, wv[rows, :])
        high, middle, low = three_parts(total[TOK:] / counts)
        spread = dot_tn(onehot, high.astype(bf16)) + dot_tn(onehot, middle.astype(bf16)) + dot_tn(onehot, low.astype(bf16))
        ref[1] = total[:TOK] + dot_nt(query_grads, wq[rows, :]) + spread


def params(vmem_bytes):
    return pltpu.CompilerParams(vmem_limit_bytes=vmem_bytes)


def vmem():
    return pl.BlockSpec(memory_space=pltpu.VMEM)


def hbm():
    return pl.BlockSpec(memory_space=pltpu.HBM)


def anywhere():
    return pl.BlockSpec(memory_space=pl.ANY)


def weight_scratch():
    return [pltpu.VMEM((D, HALF), bf16)] * 3 + [pltpu.VMEM((HALF, D), bf16)]


def shards(video, assign, w_query, w_key, w_value, w_out, cotangent):
    pair_shape = jax.ShapeDtypeStruct((LOCAL_HEADS, TOK, LANES), bf16)
    message_shape = jax.ShapeDtypeStruct((SPLITS, LOCAL_HEADS, ROWS, LANES), bf16)
    message, query_pairs, own_pairs = pl.pallas_call(
        pre_kernel,
        out_shape=(message_shape, pair_shape, pair_shape),
        in_specs=[anywhere()] * 7,
        out_specs=(hbm(), vmem(), vmem()),
        scratch_shapes=[
            pltpu.VMEM((TOK, D), bf16),
            pltpu.VMEM((1, TOK), jnp.int32),
            pltpu.VMEM((TOK, D), bf16),
            *weight_scratch(),
            pltpu.VMEM(message_shape.shape, bf16),
            pltpu.SemaphoreType.DMA((7,)),
            pltpu.SemaphoreType.DMA((LOCAL_HEADS,)),
        ],
        compiler_params=params(FIRST_VMEM),
        name="project",
    )(video[0], assign, cotangent[0], w_query, w_key, w_value, w_out)

    received = lax.all_to_all(message.reshape(CHIPS, ROWS, LANES), "tm", 0, 0, tiled=True)
    answer = pl.pallas_call(
        attend_kernel,
        out_shape=jax.ShapeDtypeStruct((CHIPS, ROWS, LANES), bf16),
        in_specs=[hbm()],
        out_specs=hbm(),
        scratch_shapes=[
            pltpu.VMEM((CHIPS, ROWS, LANES), bf16),
            pltpu.VMEM((CHIPS, ROWS, LANES), bf16),
            pltpu.VMEM((LANES, KEYS), bf16),
            pltpu.VMEM((2, KEYS, QBLOCK), f32),
            pltpu.VMEM((2, KEYS, QBLOCK), f32),
            pltpu.VMEM((KEYS, LANES), f32),
            pltpu.SemaphoreType.DMA((NBLOCKS,)),
            pltpu.SemaphoreType.DMA,
        ],
        compiler_params=params(MIDDLE_VMEM),
        name="attend",
    )(received)
    returned = lax.all_to_all(answer, "tm", 0, 0, tiled=True).reshape(message_shape.shape)

    half_shape = jax.ShapeDtypeStruct((2, TOK, HALF), f32)
    mine, other = pl.pallas_call(
        post_kernel,
        out_shape=(half_shape, half_shape),
        in_specs=[hbm()] + [vmem()] * 3 + [anywhere()] * 4,
        out_specs=(vmem(), vmem()),
        scratch_shapes=[
            *weight_scratch(),
            pltpu.VMEM(message_shape.shape, bf16),
            pltpu.SemaphoreType.DMA((4,)),
            pltpu.SemaphoreType.DMA((LOCAL_HEADS,)),
        ],
        compiler_params=params(LAST_VMEM),
        name="gradients",
    )(returned, assign, query_pairs, own_pairs, w_query, w_key, w_value, w_out)
    total = mine + lax.ppermute(other, "head", [(0, 1), (1, 0)])
    total = total.astype(bf16)
    return (total[0][None], total[1][None])


def solution(mesh):
    placed = (P("tm", None, None), P("tm", None), P(), P(), P(), P(), P("tm", None, None))
    return jax.shard_map(
        shards,
        mesh=mesh,
        in_specs=placed,
        out_specs=(P("tm", None, "head"), P("tm", None, "head")),
        check_vma=False,
    )
```

```python
import jax
import jax.numpy as jnp
from jax import lax
from jax.experimental import pallas as pl
from jax.experimental.pallas import tpu as pltpu
from jax.sharding import PartitionSpec as P

HEAD_DIM = 64
MEM = 32
TOK = 128
D = 1024
HALF = 512
HEADS = 16
CHIPS = 128
SPLITS = CHIPS // HEADS
OWN = TOK // 2
OWN_MEM = MEM // 2
QROWS = OWN // SPLITS
ROWS = OWN_MEM + 2 * QROWS
CHUNK_HEADS = 4
GROUP = 2
CHUNK = CHUNK_HEADS * HEAD_DIM
CHUNKS = HEADS // CHUNK_HEADS
LANES = 2 * HEAD_DIM
KEYS = CHIPS * MEM
BLOCK_SEGS = 16
QBLOCK = BLOCK_SEGS * QROWS
KBLOCK = BLOCK_SEGS * MEM
KHALF = KBLOCK // 2
NBLOCKS = CHIPS // BLOCK_SEGS
SCALE = 0.125
MASKED = -3e38
FIRST_VMEM = 60 * 1024 * 1024
MIDDLE_VMEM = 40 * 1024 * 1024
LAST_VMEM = 32 * 1024 * 1024
f32 = jnp.float32
bf16 = jnp.bfloat16


def dot(a, b):
    return jnp.dot(a, b, preferred_element_type=f32)


def dot_nt(a, b):
    return lax.dot_general(a, b, (((1,), (1,)), ((), ())), preferred_element_type=f32)


def dot_tn(a, b):
    return lax.dot_general(a, b, (((0,), (0,)), ((), ())), preferred_element_type=f32)


def three_parts(x):
    high = x.astype(bf16).astype(f32)
    rest = x - high
    middle = rest.astype(bf16).astype(f32)
    low = (rest - middle).astype(bf16).astype(f32)
    return high, middle, low


def low_lanes(shape):
    return lax.broadcasted_iota(jnp.int32, shape, 1) < HEAD_DIM


def split_pair(pair):
    low = low_lanes(pair.shape)
    zero = jnp.zeros_like(pair)
    return jnp.concatenate([jnp.where(low, pair, zero), jnp.where(low, zero, pair)], axis=0)


def head_cols(matrix, head):
    return matrix[:, head * HEAD_DIM : (head + 1) * HEAD_DIM]


def onehot_rows(assign_row, first):
    rows = lax.broadcasted_iota(jnp.int32, (OWN_MEM, TOK), 0) + first
    return (rows == assign_row).astype(f32)


def pre_kernel(
    tok_hbm, asg_hbm, cot_hbm, wq_hbm, wk_hbm, wv_hbm, wo_hbm, msg_hbm, qd_ref, kv_ref,
    tok_ref, asg_ref, cot_ref, wq, wk, wv, wo, msg_ref, sems, w_sems, out_sems,
):
    half = lax.axis_index("head")
    own_rows = pl.ds(pl.multiple_of(half * OWN, OWN), OWN)
    moves = [(asg_hbm, asg_ref), (tok_hbm, tok_ref), (cot_hbm.at[own_rows, :], cot_ref)]
    copies = [pltpu.make_async_copy(source, target, sems.at[at]) for at, (source, target) in enumerate(moves)]
    weights = []
    for chunk in range(CHUNKS):
        cols = slice(chunk * CHUNK, (chunk + 1) * CHUNK)
        pairs = [
            (wk_hbm.at[:, cols], wk.at[:, cols]),
            (wv_hbm.at[:, cols], wv.at[:, cols]),
            (wq_hbm.at[:, cols], wq.at[:, cols]),
            (wo_hbm.at[cols, :], wo.at[cols, :]),
        ]
        weights.append(
            [pltpu.make_async_copy(source, target, w_sems.at[chunk, at]) for at, (source, target) in enumerate(pairs)]
        )
    for copy in copies + weights[0] + weights[1]:
        copy.start()
    copies[0].wait()
    onehot = onehot_rows(asg_ref[...], half * OWN_MEM)
    counts = jnp.sum(onehot, axis=1, keepdims=True)
    copies[1].wait()
    tokens = tok_ref[...]
    memory = (dot(onehot.astype(bf16), tokens) / counts).astype(bf16)
    rows = jnp.concatenate([memory, tokens], axis=0)
    own_tokens = tok_ref[own_rows, :]
    copies[2].wait()
    own_cotangent = cot_ref[...]
    lane = lax.broadcasted_iota(jnp.int32, (OWN, LANES), 1)
    sends = []
    for chunk in range(CHUNKS):
        cols = slice(chunk * CHUNK, (chunk + 1) * CHUNK)
        for copy in weights[chunk]:
            copy.wait()
        if chunk + 2 < CHUNKS:
            for copy in weights[chunk + 2]:
                copy.start()
        keys = dot(rows, wk[:, cols]).astype(bf16)
        values = dot(rows, wv[:, cols]).astype(bf16)
        queries = (dot(own_tokens, wq[:, cols]).astype(bf16).astype(f32) * SCALE).astype(bf16)
        grad_out = dot_nt(own_cotangent, wo[cols, :]).astype(bf16)
        for at_head in range(CHUNK_HEADS):
            head = chunk * CHUNK_HEADS + at_head
            pair = jnp.concatenate([head_cols(keys, at_head), head_cols(values, at_head)], axis=1)
            query_pair = jnp.concatenate([head_cols(queries, at_head), head_cols(grad_out, at_head)], axis=1)
            kv_ref[head] = pair[OWN_MEM:]
            qd_ref[head] = query_pair
            msg_ref[:, head, :OWN_MEM, :] = jnp.broadcast_to(pair[:OWN_MEM][None], (SPLITS, OWN_MEM, LANES))
    for chunk in range(CHUNKS // GROUP):
        group = range(chunk * CHUNK_HEADS * GROUP, (chunk + 1) * CHUNK_HEADS * GROUP)
        query_pairs = [qd_ref[head] for head in group]
        low = low_lanes((OWN, LANES))
        scores = [dot_nt(jnp.where(low, q, jnp.zeros_like(q)), kv_ref[head]) for head, q in zip(group, query_pairs)]
        row_max = [jnp.max(x, axis=1, keepdims=True) for x in scores]
        raised = [jnp.exp(x - m) for x, m in zip(scores, row_max)]
        row_sum = [jnp.sum(x, axis=1, keepdims=True) for x in raised]
        sides = [dot((x / t).astype(bf16), kv_ref[head]) for head, x, t in zip(group, raised, row_sum)]
        for head, query_pair, top, total, side in zip(group, query_pairs, row_max, row_sum, sides):
            for at, part in enumerate(three_parts(top) + three_parts(total)):
                side = jnp.where(lane == at, part, side)
            msg_ref[:, head, OWN_MEM:, :] = jnp.concatenate(
                [query_pair.astype(f32).reshape(SPLITS, QROWS, LANES), side.reshape(SPLITS, QROWS, LANES)], axis=1
            ).astype(bf16)
        heads = slice(group[0], group[-1] + 1)
        sends.append(pltpu.make_async_copy(msg_ref.at[:, heads], msg_hbm.at[:, heads], out_sems.at[chunk]))
        sends[-1].start()
    for send in sends:
        send.wait()


def attend_kernel(
    msg_hbm, away_hbm, tail_hbm, mine_hbm, other_hbm,
    msg_ref, away_ref, tail_ref, mine_ref, other_ref, kvt, scores, dprobs, accum, in_sems, away_sems, out_sems,
):
    def segs(j):
        return slice(j * BLOCK_SEGS, (j + 1) * BLOCK_SEGS)

    def block(j):
        return slice(j * KBLOCK, (j + 1) * KBLOCK)

    def kv_block(j):
        near = msg_ref[segs(j), :OWN_MEM, :].reshape(KHALF, LANES)
        return jnp.concatenate([near, away_ref[segs(j)].reshape(KHALF, LANES)], axis=0)

    copies = []
    for j in range(NBLOCKS):
        copies.append(pltpu.make_async_copy(msg_hbm.at[segs(j)], msg_ref.at[segs(j)], in_sems.at[j]))
        copies.append(pltpu.make_async_copy(away_hbm.at[segs(j)], away_ref.at[segs(j)], away_sems.at[j]))
    for copy in copies:
        copy.start()
    eye = (
        lax.broadcasted_iota(jnp.int32, (LANES, LANES), 0) == lax.broadcasted_iota(jnp.int32, (LANES, LANES), 1)
    ).astype(bf16)
    visible = lax.broadcasted_iota(jnp.int32, (KBLOCK, QBLOCK), 0) % KHALF // OWN_MEM < (
        lax.broadcasted_iota(jnp.int32, (KBLOCK, QBLOCK), 1) // QROWS
    )

    def fold(op, x):
        return op(x.reshape(KBLOCK // 8, 8, QBLOCK), axis=0)

    state = [{} for _ in range(NBLOCKS)]

    def score_stage(i):
        buf, mine = i % 3, state[i]
        copies[2 * i].wait()
        copies[2 * i + 1].wait()
        kvt[:, block(i)] = dot_nt(eye, kv_block(i)).astype(bf16)
        rows = msg_ref[segs(i), OWN_MEM:, :].astype(f32)
        query_pair = rows[:, :QROWS].reshape(QBLOCK, LANES)
        side = rows[:, QROWS:].reshape(QBLOCK, LANES).T
        mine["own_out"] = side[HEAD_DIM:]
        mine["own_max"] = side[0:1] + side[1:2] + side[2:3]
        mine["own_sum"] = side[3:4] + side[4:5] + side[5:6]
        mine["grad_t"] = query_pair.T[HEAD_DIM:]
        mine["pair_rows"] = split_pair(query_pair).astype(bf16)
        top = jnp.broadcast_to(mine["own_max"], (8, QBLOCK))
        for j in range(i + 1):
            both = dot_nt(kv_block(j), mine["pair_rows"])
            score = both[:, :QBLOCK]
            if j == i:
                score = jnp.where(visible, score, MASKED)
            scores[buf, block(j), :] = score
            dprobs[buf, block(j), :] = both[:, QBLOCK:]
            top = jnp.maximum(top, fold(jnp.max, score))
            yield
        mine["row_max"] = jnp.max(top, axis=0, keepdims=True)

    def weight_stage(i):
        buf, mine = i % 3, state[i]
        row_max = mine["row_max"]
        total = jnp.zeros((8, QBLOCK), f32)
        out = jnp.zeros((LANES, QBLOCK), f32)
        for j in range(i + 1):
            raised = jnp.exp(scores[buf, block(j), :] - row_max)
            scores[buf, block(j), :] = raised
            total = total + fold(jnp.sum, raised)
            out = out + dot(kvt[:, block(j)], raised.astype(bf16))
            yield
        own_share = mine["own_sum"] * jnp.exp(mine["own_max"] - row_max)
        row_sum = own_share + jnp.sum(total, axis=0, keepdims=True)
        inverse = 1.0 / row_sum
        heads_out = ((mine["own_out"] * own_share + out[HEAD_DIM:]) * inverse).astype(bf16).astype(f32)
        mine.update(row_sum=row_sum, inverse=inverse, heads_out=heads_out)
        mine["delta"] = jnp.sum(mine["grad_t"] * heads_out, axis=0, keepdims=True)

    def grad_stage(i):
        buf, mine = i % 3, state[i]
        grad = jnp.zeros((LANES, QBLOCK), f32)
        for j in range(i + 1):
            probs = scores[buf, block(j), :] * mine["inverse"]
            dscores = (probs * (dprobs[buf, block(j), :] - mine["delta"])).astype(bf16)
            both = jnp.concatenate([dscores, probs.astype(bf16)], axis=1)
            term = dot(both, mine["pair_rows"])
            if j == i:
                accum[block(j), :] = term
            else:
                accum[block(j), :] += term
            grad = grad + dot(kvt[:, block(j)], dscores)
            yield
        query_grad = grad[:HEAD_DIM]
        grad_high = query_grad.astype(bf16).astype(f32)
        main = jnp.concatenate([grad_high, mine["heads_out"]], axis=0).T
        row_at = lax.broadcasted_iota(jnp.int32, (HEAD_DIM, QBLOCK), 0)
        stats = jnp.zeros((HEAD_DIM, QBLOCK), f32)
        for at, part in enumerate(three_parts(mine["row_max"]) + three_parts(mine["row_sum"])):
            stats = jnp.where(row_at == at, part, stats)
        extra = jnp.concatenate([query_grad - grad_high, stats], axis=0).T
        tail_ref[segs(i)] = jnp.concatenate(
            [main.reshape(BLOCK_SEGS, QROWS, LANES), extra.reshape(BLOCK_SEGS, QROWS, LANES)], axis=1
        ).astype(bf16)

    for step in range(NBLOCKS + 2):
        running = []
        for at, stage in ((step - 2, grad_stage), (step - 1, weight_stage), (step, score_stage)):
            if 0 <= at < NBLOCKS:
                running.append(stage(at))
        while running:
            for one in list(running):
                if next(one, one) is one:
                    running.remove(one)

    sends = [pltpu.make_async_copy(tail_ref, tail_hbm, out_sems.at[0])]
    sends[0].start()
    for j in range(NBLOCKS):
        total = accum[block(j), :]
        mine_ref[segs(j)] = total[:KHALF].reshape(BLOCK_SEGS, OWN_MEM, LANES)
        other_ref[segs(j)] = total[KHALF:].astype(bf16).reshape(BLOCK_SEGS, OWN_MEM, LANES)
    sends.append(pltpu.make_async_copy(mine_ref, mine_hbm, out_sems.at[1]))
    sends.append(pltpu.make_async_copy(other_ref, other_hbm, out_sems.at[2]))
    sends[1].start()
    sends[2].start()
    for send in sends:
        send.wait()


def post_kernel(
    msg_hbm, asg_ref, qd_ref, kv_ref, wq, wk, wv, wo, out_ref, mine_ref, other_ref, msg_ref, in_sems,
):
    half = lax.axis_index("head")
    offset = pl.multiple_of(half * HALF, HALF)
    away = pl.multiple_of((1 - half) * HALF, HALF)
    parts = [
        pltpu.make_async_copy(msg_hbm.at[:, head], msg_ref.at[:, head], in_sems.at[head]) for head in range(HEADS)
    ]
    for copy in parts:
        copy.start()
    onehot = onehot_rows(asg_ref[...], half * OWN_MEM)
    counts = jnp.sum(onehot, axis=1, keepdims=True)
    onehot = onehot.astype(bf16)
    for copy in parts:
        copy.wait()
    heads = range(HEADS)
    mem_pairs = [jnp.sum(msg_ref[:, head, :OWN_MEM, :].astype(f32), axis=0) for head in heads]
    pair_rows = [split_pair(qd_ref[head]) for head in heads]
    both = [dot_nt(pair_rows[head], kv_ref[head]) for head in heads]
    rows = [msg_ref[:, head, OWN_MEM:, :].astype(f32) for head in heads]
    mains = [x[:, :QROWS].reshape(OWN, LANES) for x in rows]
    extras = [x[:, QROWS:].reshape(OWN, LANES) for x in rows]
    at = HEAD_DIM
    row_max = [x[:, at : at + 1] + x[:, at + 1 : at + 2] + x[:, at + 2 : at + 3] for x in extras]
    row_sum = [x[:, at + 3 : at + 4] + x[:, at + 4 : at + 5] + x[:, at + 5 : at + 6] for x in extras]
    products = [qd_ref[head].astype(f32) * mains[head] for head in heads]
    deltas = [jnp.sum(jnp.where(low_lanes(x.shape), 0.0, x), axis=1, keepdims=True) for x in products]
    probs = [jnp.exp(both[head][:OWN] - row_max[head]) / row_sum[head] for head in heads]
    dscores = [(probs[head] * (both[head][OWN:] - deltas[head])).astype(bf16) for head in heads]
    own_grads = [dot(dscores[head], kv_ref[head]) for head in heads]
    own_pairs = [
        dot_tn(jnp.concatenate([dscores[head], probs[head].astype(bf16)], axis=0), pair_rows[head]) for head in heads
    ]
    grads = [jnp.concatenate([own_pairs[head], mem_pairs[head]], axis=0) for head in heads]
    heads_out = [x[:, HEAD_DIM:] for x in mains]
    query_grads = [((mains[head] + extras[head] + own_grads[head]) * SCALE)[:, :HEAD_DIM] for head in heads]
    key_grads = [x[:, :HEAD_DIM] for x in grads]
    value_grads = [x[:, HEAD_DIM:] for x in grads]

    def merge(parts):
        return jnp.concatenate(parts, axis=1).astype(bf16)

    heads_out = merge(heads_out)
    query_grads = merge(query_grads)
    key_grads = merge(key_grads)
    value_grads = merge(value_grads)
    own_rows = pl.ds(pl.multiple_of(half * OWN, OWN), OWN)
    for start, keep in ((away, False), (offset, True)):
        rows = pl.ds(start, HALF)
        attended = dot(heads_out, wo[:, rows])
        total = dot_nt(key_grads, wk[rows, :]) + dot_nt(value_grads, wv[rows, :])
        high, middle, low = three_parts(total[TOK:] / counts)
        spread = dot_tn(onehot, high.astype(bf16)) + dot_tn(onehot, middle.astype(bf16)) + dot_tn(onehot, low.astype(bf16))
        grad_rows = pl.ds(0, TOK)
        if keep:
            out_ref[...] = attended
            mine_ref[...] = total[:TOK] + spread
            mine_ref[own_rows, :] += dot_nt(query_grads, wq[rows, :])
        else:
            other_ref[grad_rows, :] = total[:TOK] + spread
            other_ref[own_rows, :] += dot_nt(query_grads, wq[rows, :])
            other_ref[TOK:, :] = attended


def params(vmem_bytes):
    return pltpu.CompilerParams(vmem_limit_bytes=vmem_bytes)


def vmem():
    return pl.BlockSpec(memory_space=pltpu.VMEM)


def hbm():
    return pl.BlockSpec(memory_space=pltpu.HBM)


def anywhere():
    return pl.BlockSpec(memory_space=pl.ANY)


def swap_cores(x):
    return lax.ppermute(x, "head", [(0, 1), (1, 0)])


def shards(video, assign, w_query, w_key, w_value, w_out, cotangent):
    message_shape = (SPLITS, HEADS, ROWS, LANES)
    message, query_pairs, own_pairs = pl.pallas_call(
        pre_kernel,
        out_shape=(
            jax.ShapeDtypeStruct(message_shape, bf16),
            jax.ShapeDtypeStruct((HEADS, OWN, LANES), bf16),
            jax.ShapeDtypeStruct((HEADS, TOK, LANES), bf16),
        ),
        in_specs=[anywhere()] * 7,
        out_specs=(hbm(), vmem(), vmem()),
        scratch_shapes=[
            pltpu.VMEM((TOK, D), bf16),
            pltpu.VMEM((1, TOK), jnp.int32),
            pltpu.VMEM((OWN, D), bf16),
            *[pltpu.VMEM((D, D), bf16)] * 4,
            pltpu.VMEM(message_shape, bf16),
            pltpu.SemaphoreType.DMA((3,)),
            pltpu.SemaphoreType.DMA((CHUNKS, 4)),
            pltpu.SemaphoreType.DMA((CHUNKS,)),
        ],
        compiler_params=params(FIRST_VMEM),
        name="project",
    )(video[0], assign, cotangent[0], w_query, w_key, w_value, w_out)

    received = lax.all_to_all(message.reshape(CHIPS, ROWS, LANES), "tm", 0, 0, tiled=True)
    away = swap_cores(received[:, :OWN_MEM])
    part_shape = (CHIPS, OWN_MEM, LANES)
    tail, mine, other = pl.pallas_call(
        attend_kernel,
        out_shape=(
            jax.ShapeDtypeStruct(part_shape, bf16),
            jax.ShapeDtypeStruct(part_shape, f32),
            jax.ShapeDtypeStruct(part_shape, bf16),
        ),
        in_specs=[hbm(), hbm()],
        out_specs=(hbm(), hbm(), hbm()),
        scratch_shapes=[
            pltpu.VMEM((CHIPS, ROWS, LANES), bf16),
            pltpu.VMEM(part_shape, bf16),
            pltpu.VMEM(part_shape, bf16),
            pltpu.VMEM(part_shape, f32),
            pltpu.VMEM(part_shape, bf16),
            pltpu.VMEM((LANES, KEYS), bf16),
            pltpu.VMEM((3, KEYS, QBLOCK), f32),
            pltpu.VMEM((3, KEYS, QBLOCK), f32),
            pltpu.VMEM((KEYS, LANES), f32),
            pltpu.SemaphoreType.DMA((NBLOCKS,)),
            pltpu.SemaphoreType.DMA((NBLOCKS,)),
            pltpu.SemaphoreType.DMA((3,)),
        ],
        compiler_params=params(MIDDLE_VMEM),
        name="attend",
    )(received, away)
    sums = (mine + swap_cores(other).astype(f32)).astype(bf16)
    answer = jnp.concatenate([sums, tail], axis=1)
    returned = lax.all_to_all(answer, "tm", 0, 0, tiled=True).reshape(message_shape)

    attended, mine, other = pl.pallas_call(
        post_kernel,
        out_shape=(
            jax.ShapeDtypeStruct((OWN, HALF), f32),
            jax.ShapeDtypeStruct((TOK, HALF), f32),
            jax.ShapeDtypeStruct((TOK + OWN, HALF), f32),
        ),
        in_specs=[hbm()] + [vmem()] * 7,
        out_specs=(vmem(), vmem(), vmem()),
        scratch_shapes=[pltpu.VMEM(message_shape, bf16), pltpu.SemaphoreType.DMA((HEADS,))],
        compiler_params=params(LAST_VMEM),
        name="gradients",
    )(returned, assign, query_pairs, own_pairs, w_query, w_key, w_value, w_out)
    arrived = swap_cores(other)
    video_grad = (mine + arrived[:TOK]).astype(bf16)
    first = lax.axis_index("head") == 0
    far = arrived[TOK:]
    upper = jnp.where(first, attended, far)
    lower = jnp.where(first, far, attended)
    attended = jnp.concatenate([upper, lower], axis=0).astype(bf16)
    return (attended[None], video_grad[None])


def solution(mesh):
    placed = (P("tm", None, None), P("tm", None), P(), P(), P(), P(), P("tm", None, None))
    return jax.shard_map(
        shards,
        mesh=mesh,
        in_specs=placed,
        out_specs=(P("tm", None, "head"), P("tm", None, "head")),
        check_vma=False,
    )
```

```python
import jax
import jax.numpy as jnp
from jax import lax
from jax.experimental import pallas as pl
from jax.experimental.pallas import tpu as pltpu
from jax.sharding import PartitionSpec as P

HEAD_DIM = 64
MEM = 32
TOK = 128
D = 1024
HALF = 512
HEADS = 16
CHIPS = 128
SPLITS = CHIPS // HEADS
OWN = TOK // 2
OWN_MEM = MEM // 2
QROWS = OWN // SPLITS
MEM_PAIRS = OWN_MEM // 2
QUERY_PAIRS = QROWS // 2
PAIRS = MEM_PAIRS + QUERY_PAIRS + 1
STATS_AT = MEM_PAIRS + QUERY_PAIRS
CHUNK_HEADS = 4
GROUP = 2
CHUNK = CHUNK_HEADS * HEAD_DIM
CHUNKS = HEADS // CHUNK_HEADS
LANES = 2 * HEAD_DIM
KEYS = CHIPS * MEM
BLOCK_SEGS = 16
QBLOCK = BLOCK_SEGS * QROWS
KBLOCK = BLOCK_SEGS * MEM
KHALF = KBLOCK // 2
NBLOCKS = CHIPS // BLOCK_SEGS
SCALE = 0.125
MASKED = -3e38
FIRST_VMEM = 60 * 1024 * 1024
MIDDLE_VMEM = 40 * 1024 * 1024
LAST_VMEM = 45 * 1024 * 1024
f32 = jnp.float32
bf16 = jnp.bfloat16


def dot(a, b):
    return jnp.dot(a, b, preferred_element_type=f32)


def dot_nt(a, b):
    return lax.dot_general(a, b, (((1,), (1,)), ((), ())), preferred_element_type=f32)


def dot_tn(a, b):
    return lax.dot_general(a, b, (((0,), (0,)), ((), ())), preferred_element_type=f32)


def three_parts(x):
    high = x.astype(bf16).astype(f32)
    rest = x - high
    middle = rest.astype(bf16).astype(f32)
    low = (rest - middle).astype(bf16).astype(f32)
    return high, middle, low


def low_lanes(shape):
    return lax.broadcasted_iota(jnp.int32, shape, 1) < HEAD_DIM


def split_pair(pair):
    low = low_lanes(pair.shape)
    zero = jnp.zeros_like(pair)
    return jnp.concatenate([jnp.where(low, pair, zero), jnp.where(low, zero, pair)], axis=0)


def head_cols(matrix, head):
    return matrix[:, head * HEAD_DIM : (head + 1) * HEAD_DIM]


def onehot_rows(assign_row, first):
    rows = lax.broadcasted_iota(jnp.int32, (OWN_MEM, TOK), 0) + first
    return (rows == assign_row).astype(f32)


def pre_kernel(
    tok_hbm, asg_hbm, cot_hbm, wq_hbm, wk_hbm, wv_hbm, wo_hbm, msg_hbm, qd_hbm, kv_hbm, side_hbm,
    tok_ref, asg_ref, cot_ref, wq, wk, wv, wo, msg_ref, qd_ref, kv_ref, side_ref, sems, w_sems, out_sems,
):
    half = lax.axis_index("head")
    own_rows = pl.ds(pl.multiple_of(half * OWN, OWN), OWN)
    moves = [(asg_hbm, asg_ref), (tok_hbm, tok_ref), (cot_hbm.at[own_rows, :], cot_ref)]
    copies = [pltpu.make_async_copy(source, target, sems.at[at]) for at, (source, target) in enumerate(moves)]
    weights = []
    for chunk in range(CHUNKS):
        cols = slice(chunk * CHUNK, (chunk + 1) * CHUNK)
        pairs = [
            (wk_hbm.at[:, cols], wk.at[:, cols]),
            (wv_hbm.at[:, cols], wv.at[:, cols]),
            (wq_hbm.at[:, cols], wq.at[:, cols]),
            (wo_hbm.at[cols, :], wo.at[cols, :]),
        ]
        weights.append(
            [pltpu.make_async_copy(source, target, w_sems.at[chunk, at]) for at, (source, target) in enumerate(pairs)]
        )
    for copy in copies + weights[0] + weights[1]:
        copy.start()
    copies[0].wait()
    onehot = onehot_rows(asg_ref[...], half * OWN_MEM)
    counts = jnp.sum(onehot, axis=1, keepdims=True)
    copies[1].wait()
    tokens = tok_ref[...]
    memory = (dot(onehot.astype(bf16), tokens) / counts).astype(bf16)
    rows = jnp.concatenate([memory, tokens], axis=0)
    own_tokens = tok_ref[own_rows, :]
    copies[2].wait()
    own_cotangent = cot_ref[...]
    lane = lax.broadcasted_iota(jnp.int32, (OWN, LANES), 1)
    sublane = lax.broadcasted_iota(jnp.int32, (OWN, LANES), 0)
    sends = []
    for chunk in range(CHUNKS):
        cols = slice(chunk * CHUNK, (chunk + 1) * CHUNK)
        for copy in weights[chunk]:
            copy.wait()
        if chunk + 2 < CHUNKS:
            for copy in weights[chunk + 2]:
                copy.start()
        keys = dot(rows, wk[:, cols]).astype(bf16)
        values = dot(rows, wv[:, cols]).astype(bf16)
        queries = (dot(own_tokens, wq[:, cols]).astype(bf16).astype(f32) * SCALE).astype(bf16)
        grad_out = dot_nt(own_cotangent, wo[cols, :]).astype(bf16)
        for at_head in range(CHUNK_HEADS):
            head = chunk * CHUNK_HEADS + at_head
            pair = jnp.concatenate([head_cols(keys, at_head), head_cols(values, at_head)], axis=1)
            query_pair = jnp.concatenate([head_cols(queries, at_head), head_cols(grad_out, at_head)], axis=1)
            kv_ref[head] = pair[OWN_MEM:]
            qd_ref[head] = query_pair
            mem_pairs = pair[:OWN_MEM].reshape(MEM_PAIRS, 2, LANES)
            msg_ref[:, head, :MEM_PAIRS] = jnp.broadcast_to(mem_pairs[None], (SPLITS, MEM_PAIRS, 2, LANES))
            msg_ref[:, head, MEM_PAIRS:STATS_AT] = query_pair.reshape(SPLITS, QUERY_PAIRS, 2, LANES)
        heads = slice(chunk * CHUNK_HEADS, (chunk + 1) * CHUNK_HEADS)
        sends.append(pltpu.make_async_copy(kv_ref.at[heads], kv_hbm.at[heads], out_sems.at[0, chunk]))
        sends.append(pltpu.make_async_copy(qd_ref.at[heads], qd_hbm.at[heads], out_sems.at[1, chunk]))
        sends[-2].start()
        sends[-1].start()
    for chunk in range(CHUNKS // GROUP):
        group = range(chunk * CHUNK_HEADS * GROUP, (chunk + 1) * CHUNK_HEADS * GROUP)
        query_pairs = [qd_ref[head] for head in group]
        low = low_lanes((OWN, LANES))
        scores = [dot_nt(jnp.where(low, q, jnp.zeros_like(q)), kv_ref[head]) for head, q in zip(group, query_pairs)]
        row_max = [jnp.max(x, axis=1, keepdims=True) for x in scores]
        raised = [jnp.exp(x - m) for x, m in zip(scores, row_max)]
        row_sum = [jnp.sum(x, axis=1, keepdims=True) for x in raised]
        sides = [dot((x / t).astype(bf16), kv_ref[head]) for head, x, t in zip(group, raised, row_sum)]
        for head, query_pair, top, total, side in zip(group, query_pairs, row_max, row_sum, sides):
            log_sum = top + jnp.log(total)
            products = jnp.where(low, 0.0, query_pair.astype(f32) * side)
            delta = jnp.sum(products, axis=1, keepdims=True)
            side_ref[head] = jnp.where(low, log_sum, side)
            stats = jnp.zeros((OWN, LANES), f32)
            for at, part in enumerate(three_parts(log_sum) + three_parts(delta)):
                stats = jnp.where(lane // QROWS == at, part, stats)
            stats = jnp.where(lane % QROWS == sublane % QROWS, stats, 0.0)
            stats = jnp.sum(stats.reshape(SPLITS, QROWS, LANES), axis=1, keepdims=True)
            msg_ref[:, head, STATS_AT] = jnp.broadcast_to(stats, (SPLITS, 2, LANES)).astype(bf16)
        heads = slice(group[0], group[-1] + 1)
        sends.append(pltpu.make_async_copy(msg_ref.at[:, heads], msg_hbm.at[:, heads], out_sems.at[2, chunk]))
        sends.append(pltpu.make_async_copy(side_ref.at[heads], side_hbm.at[heads], out_sems.at[3, chunk]))
        sends[-2].start()
        sends[-1].start()
    for send in sends:
        send.wait()


def attend_kernel(msg_ref, away_ref, tail_ref, mine_ref, other_ref, kv, kvt, scores, dprobs, accum):
    def segs(j):
        return slice(j * BLOCK_SEGS, (j + 1) * BLOCK_SEGS)

    def block(j):
        return slice(j * KBLOCK, (j + 1) * KBLOCK)

    def kv_block(j):
        return kv[block(j), :]

    eye = (
        lax.broadcasted_iota(jnp.int32, (LANES, LANES), 0) == lax.broadcasted_iota(jnp.int32, (LANES, LANES), 1)
    ).astype(bf16)
    visible = lax.broadcasted_iota(jnp.int32, (KBLOCK, QBLOCK), 0) % KHALF // OWN_MEM < (
        lax.broadcasted_iota(jnp.int32, (KBLOCK, QBLOCK), 1) // QROWS
    )

    def fold(op, x):
        return op(x.reshape(KBLOCK // 8, 8, QBLOCK), axis=0)

    row = lax.broadcasted_iota(jnp.int32, (2 * BLOCK_SEGS, QBLOCK), 0)
    column = lax.broadcasted_iota(jnp.int32, (2 * BLOCK_SEGS, QBLOCK), 1)
    spread = (row == column // QROWS * 2).astype(bf16)
    square_row = lax.broadcasted_iota(jnp.int32, (LANES, LANES), 0)
    square_column = lax.broadcasted_iota(jnp.int32, (LANES, LANES), 1)
    same_query = square_row % QROWS == square_column % QROWS
    gather = (
        lax.broadcasted_iota(jnp.int32, (8, LANES), 0) == lax.broadcasted_iota(jnp.int32, (8, LANES), 1) // QROWS
    ).astype(bf16)
    blocks = range(NBLOCKS)
    stats = [dot_tn(spread, msg_ref[segs(i), STATS_AT].reshape(2 * BLOCK_SEGS, LANES)) for i in blocks]
    stats = [dot_nt(gather, jnp.where(same_query, x, 0.0).astype(bf16)) for x in stats]
    state = [
        {"own_log": x[0:1] + x[1:2] + x[2:3], "own_delta": x[3:4] + x[4:5] + x[5:6]} for x in stats
    ]

    def score_stage(i):
        buf, mine = i % 3, state[i]
        kv[i * KBLOCK : i * KBLOCK + KHALF, :] = msg_ref[segs(i), :MEM_PAIRS].reshape(KHALF, LANES)
        kv[i * KBLOCK + KHALF : (i + 1) * KBLOCK, :] = away_ref[segs(i)].reshape(KHALF, LANES)
        kvt[:, block(i)] = dot_nt(eye, kv_block(i)).astype(bf16)
        query_pair = msg_ref[segs(i), MEM_PAIRS:STATS_AT].reshape(QBLOCK, LANES).astype(f32)
        mine["grad_t"] = query_pair.T[HEAD_DIM:]
        mine["pair_rows"] = split_pair(query_pair).astype(bf16)
        top = jnp.full((8, QBLOCK), MASKED, f32)
        for j in range(i + 1):
            both = dot_nt(kv_block(j), mine["pair_rows"])
            score = both[:, :QBLOCK]
            if j == i:
                score = jnp.where(visible, score, MASKED)
            scores[buf, block(j), :] = score
            dprobs[buf, block(j), :] = both[:, QBLOCK:]
            top = jnp.maximum(top, fold(jnp.max, score))
            yield
        mine["row_max"] = jnp.maximum(jnp.max(top, axis=0, keepdims=True), mine["own_log"])

    def weight_stage(i):
        buf, mine = i % 3, state[i]
        row_max = mine["row_max"]
        total = jnp.zeros((8, QBLOCK), f32)
        out = jnp.zeros((LANES, QBLOCK), f32)
        for j in range(i + 1):
            raised = jnp.exp(scores[buf, block(j), :] - row_max)
            scores[buf, block(j), :] = raised
            total = total + fold(jnp.sum, raised)
            out = out + dot(kvt[:, block(j)], raised.astype(bf16))
            yield
        own_share = jnp.exp(mine["own_log"] - row_max)
        row_sum = own_share + jnp.sum(total, axis=0, keepdims=True)
        inverse = 1.0 / row_sum
        out = out[HEAD_DIM:] * inverse
        mine.update(log_sum=row_max + jnp.log(row_sum), inverse=inverse, out=out)
        mine["delta"] = jnp.sum(mine["grad_t"] * out, axis=0, keepdims=True) + own_share * inverse * mine["own_delta"]

    def grad_stage(i):
        buf, mine = i % 3, state[i]
        grad = jnp.zeros((LANES, QBLOCK), f32)
        for j in range(i + 1):
            probs = scores[buf, block(j), :] * mine["inverse"]
            dscores = (probs * (dprobs[buf, block(j), :] - mine["delta"])).astype(bf16)
            both = jnp.concatenate([dscores, probs.astype(bf16)], axis=1)
            term = dot(both, mine["pair_rows"])
            if j < i:
                term = accum[block(j), :] + term
            if i < NBLOCKS - 1:
                accum[block(j), :] = term
            else:
                mine_ref[j * KHALF : (j + 1) * KHALF, :] = term[:KHALF]
                other_ref[segs(j)] = term[KHALF:].astype(bf16).reshape(BLOCK_SEGS, MEM_PAIRS, 2, LANES)
            grad = grad + dot(kvt[:, block(j)], dscores)
            yield
        main = jnp.concatenate([grad[:HEAD_DIM], mine["out"]], axis=0).T.astype(bf16)
        tail_ref[segs(i), :QUERY_PAIRS] = main.reshape(BLOCK_SEGS, QUERY_PAIRS, 2, LANES)

    for step in range(NBLOCKS + 2):
        running = []
        for at, stage in ((step - 2, grad_stage), (step - 1, weight_stage), (step, score_stage)):
            if 0 <= at < NBLOCKS:
                running.append(stage(at))
        while running:
            for one in list(running):
                if next(one, one) is one:
                    running.remove(one)

    stats = [jnp.zeros((LANES, LANES), f32) for _ in blocks]
    for at in range(3):
        parts = [three_parts(one["log_sum"])[at] for one in state]
        stats = [jnp.where(square_row // QROWS == at, part, x) for part, x in zip(parts, stats)]
    stats = [dot_nt(spread, jnp.where(same_query, x, 0.0).astype(bf16)) for x in stats]
    for i in blocks:
        tail_ref[segs(i), QUERY_PAIRS] = stats[i].astype(bf16).reshape(BLOCK_SEGS, 2, LANES)


def join_kernel(mine_ref, other_ref, tail_ref, out_ref):
    out_ref[:, MEM_PAIRS:] = tail_ref[...]
    for j in range(NBLOCKS):
        segs = slice(j * BLOCK_SEGS, (j + 1) * BLOCK_SEGS)
        far = other_ref[segs].reshape(KHALF, LANES).astype(f32)
        total = (mine_ref[j * KHALF : (j + 1) * KHALF, :] + far).astype(bf16)
        out_ref[segs, :MEM_PAIRS] = total.reshape(BLOCK_SEGS, MEM_PAIRS, 2, LANES)


def post_kernel(
    msg_ref, asg_ref, qd_ref, kv_ref, side_ref, wq, wk, wv, wo_hbm, out_ref, mine_ref, other_ref, wo, wo_sem,
):
    half = lax.axis_index("head")
    offset = pl.multiple_of(half * HALF, HALF)
    away = pl.multiple_of((1 - half) * HALF, HALF)
    wo_copy = pltpu.make_async_copy(wo_hbm, wo, wo_sem)
    wo_copy.start()
    onehot = onehot_rows(asg_ref[...], half * OWN_MEM)
    counts = jnp.sum(onehot, axis=1, keepdims=True)
    onehot = onehot.astype(bf16)
    heads = range(HEADS)
    def mem_sum(head):
        parts = [msg_ref[k, head, :MEM_PAIRS].reshape(OWN_MEM, LANES).astype(f32) for k in range(SPLITS)]
        return sum(parts[1:], parts[0])

    mem_pairs = [mem_sum(head) for head in heads]
    pair_rows = [split_pair(qd_ref[head]) for head in heads]
    both = [dot_nt(pair_rows[head], kv_ref[head]) for head in heads]
    returned = [msg_ref[:, head, MEM_PAIRS:STATS_AT].reshape(OWN, LANES).astype(f32) for head in heads]
    sublane = lax.broadcasted_iota(jnp.int32, (OWN, LANES), 0)
    lane = lax.broadcasted_iota(jnp.int32, (OWN, LANES), 1)
    same_query = sublane % QROWS == lane % QROWS

    def log_sum_of(head):
        stats = msg_ref[:, head, STATS_AT].astype(f32)[:, :1]
        stats = jnp.broadcast_to(stats, (SPLITS, QROWS, LANES)).reshape(OWN, LANES)
        return jnp.sum(jnp.where(same_query, stats, 0.0), axis=1, keepdims=True)

    log_sums = [log_sum_of(head) for head in heads]
    shares = [jnp.exp(side_ref[head][:, :1] - log_sums[head]) for head in heads]
    mains = [(returned[head] + shares[head] * side_ref[head]).astype(bf16).astype(f32) for head in heads]
    products = [qd_ref[head].astype(f32) * mains[head] for head in heads]
    deltas = [jnp.sum(jnp.where(low_lanes(x.shape), 0.0, x), axis=1, keepdims=True) for x in products]
    probs = [jnp.exp(both[head][:OWN] - log_sums[head]) for head in heads]
    dscores = [(probs[head] * (both[head][OWN:] - deltas[head])).astype(bf16) for head in heads]
    own_grads = [dot(dscores[head], kv_ref[head]) for head in heads]
    own_pairs = [
        dot_tn(jnp.concatenate([dscores[head], probs[head].astype(bf16)], axis=0), pair_rows[head]) for head in heads
    ]
    grads = [jnp.concatenate([own_pairs[head], mem_pairs[head]], axis=0) for head in heads]
    heads_out = [x[:, HEAD_DIM:] for x in mains]
    query_grads = [((returned[head] + own_grads[head]) * SCALE)[:, :HEAD_DIM] for head in heads]
    key_grads = [x[:, :HEAD_DIM] for x in grads]
    value_grads = [x[:, HEAD_DIM:] for x in grads]

    def merge(parts):
        return jnp.concatenate(parts, axis=1).astype(bf16)

    heads_out = merge(heads_out)
    query_grads = merge(query_grads)
    key_grads = merge(key_grads)
    value_grads = merge(value_grads)
    own_rows = pl.ds(pl.multiple_of(half * OWN, OWN), OWN)
    for start, keep in ((away, False), (offset, True)):
        rows = pl.ds(start, HALF)
        total = dot_nt(key_grads, wk[rows, :]) + dot_nt(value_grads, wv[rows, :])
        high, middle, low = three_parts(total[TOK:] / counts)
        spread = dot_tn(onehot, high.astype(bf16)) + dot_tn(onehot, middle.astype(bf16)) + dot_tn(onehot, low.astype(bf16))
        grad_rows = pl.ds(0, TOK)
        if keep:
            mine_ref[...] = total[:TOK] + spread
            mine_ref[own_rows, :] += dot_nt(query_grads, wq[rows, :])
        else:
            other_ref[grad_rows, :] = total[:TOK] + spread
            other_ref[own_rows, :] += dot_nt(query_grads, wq[rows, :])
    wo_copy.wait()
    other_ref[TOK:, :] = dot(heads_out, wo[:, pl.ds(away, HALF)])
    out_ref[...] = dot(heads_out, wo[:, pl.ds(offset, HALF)])


def finish_kernel(attended_ref, mine_ref, arrived_ref, out_ref, grad_ref):
    half = lax.axis_index("head")
    own_rows = pl.ds(pl.multiple_of(half * OWN, OWN), OWN)
    far_rows = pl.ds(pl.multiple_of((1 - half) * OWN, OWN), OWN)
    out_ref[0, own_rows, :] = attended_ref[...].astype(bf16)
    out_ref[0, far_rows, :] = arrived_ref[TOK:, :].astype(bf16)
    grad_ref[0] = (mine_ref[...] + arrived_ref[:TOK, :]).astype(bf16)


def params(vmem_bytes):
    return pltpu.CompilerParams(vmem_limit_bytes=vmem_bytes)


def vmem():
    return pl.BlockSpec(memory_space=pltpu.VMEM)


def hbm():
    return pl.BlockSpec(memory_space=pltpu.HBM)


def anywhere():
    return pl.BlockSpec(memory_space=pl.ANY)


def swap_cores(x):
    return lax.ppermute(x, "head", [(0, 1), (1, 0)])


def shards(video, assign, w_query, w_key, w_value, w_out, cotangent):
    message_shape = (SPLITS, HEADS, PAIRS, 2, LANES)
    chip_shape = (CHIPS, PAIRS, 2, LANES)
    message, query_pairs, own_pairs, own_sides = pl.pallas_call(
        pre_kernel,
        out_shape=(
            jax.ShapeDtypeStruct(message_shape, bf16),
            jax.ShapeDtypeStruct((HEADS, OWN, LANES), bf16),
            jax.ShapeDtypeStruct((HEADS, TOK, LANES), bf16),
            jax.ShapeDtypeStruct((HEADS, OWN, LANES), f32),
        ),
        in_specs=[anywhere()] * 7,
        out_specs=(hbm(), hbm(), hbm(), hbm()),
        scratch_shapes=[
            pltpu.VMEM((TOK, D), bf16),
            pltpu.VMEM((1, TOK), jnp.int32),
            pltpu.VMEM((OWN, D), bf16),
            *[pltpu.VMEM((D, D), bf16)] * 4,
            pltpu.VMEM(message_shape, bf16),
            pltpu.VMEM((HEADS, OWN, LANES), bf16),
            pltpu.VMEM((HEADS, TOK, LANES), bf16),
            pltpu.VMEM((HEADS, OWN, LANES), f32),
            pltpu.SemaphoreType.DMA((3,)),
            pltpu.SemaphoreType.DMA((CHUNKS, 4)),
            pltpu.SemaphoreType.DMA((4, CHUNKS)),
        ],
        compiler_params=params(FIRST_VMEM),
        name="project",
    )(video[0], assign, cotangent[0], w_query, w_key, w_value, w_out)

    received = lax.all_to_all(message.reshape(chip_shape), "tm", 0, 0, tiled=True)
    away = swap_cores(received[:, :MEM_PAIRS])
    part_shape = (CHIPS, MEM_PAIRS, 2, LANES)
    tail_shape = (CHIPS, PAIRS - MEM_PAIRS, 2, LANES)
    mine_shape = (CHIPS * OWN_MEM, LANES)
    tail, mine, other = pl.pallas_call(
        attend_kernel,
        out_shape=(
            jax.ShapeDtypeStruct(tail_shape, bf16),
            jax.ShapeDtypeStruct(mine_shape, f32),
            jax.ShapeDtypeStruct(part_shape, bf16),
        ),
        in_specs=[vmem(), vmem()],
        out_specs=(vmem(), vmem(), vmem()),
        scratch_shapes=[
            pltpu.VMEM((KEYS, LANES), bf16),
            pltpu.VMEM((LANES, KEYS), bf16),
            pltpu.VMEM((3, KEYS, QBLOCK), f32),
            pltpu.VMEM((3, KEYS, QBLOCK), f32),
            pltpu.VMEM((KEYS, LANES), f32),
        ],
        compiler_params=params(MIDDLE_VMEM),
        name="attend",
    )(received, away)
    answer = pl.pallas_call(
        join_kernel,
        out_shape=jax.ShapeDtypeStruct(chip_shape, bf16),
        in_specs=[vmem()] * 3,
        out_specs=vmem(),
        compiler_params=params(LAST_VMEM),
        name="join",
    )(mine, swap_cores(other), tail)
    returned = lax.all_to_all(answer, "tm", 0, 0, tiled=True).reshape(message_shape)

    attended, mine, other = pl.pallas_call(
        post_kernel,
        out_shape=(
            jax.ShapeDtypeStruct((OWN, HALF), f32),
            jax.ShapeDtypeStruct((TOK, HALF), f32),
            jax.ShapeDtypeStruct((TOK + OWN, HALF), f32),
        ),
        in_specs=[vmem()] * 8 + [anywhere()],
        out_specs=(vmem(), vmem(), vmem()),
        scratch_shapes=[pltpu.VMEM((D, D), bf16), pltpu.SemaphoreType.DMA],
        compiler_params=params(LAST_VMEM),
        name="gradients",
    )(returned, assign, query_pairs, own_pairs, own_sides, w_query, w_key, w_value, w_out)
    half_shape = jax.ShapeDtypeStruct((1, TOK, HALF), bf16)
    return pl.pallas_call(
        finish_kernel,
        out_shape=(half_shape, half_shape),
        in_specs=[vmem()] * 3,
        out_specs=(vmem(), vmem()),
        compiler_params=params(LAST_VMEM),
        name="finish",
    )(attended, mine, swap_cores(other))


def solution(mesh):
    placed = (P("tm", None, None), P("tm", None), P(), P(), P(), P(), P("tm", None, None))
    return jax.shard_map(
        shards,
        mesh=mesh,
        in_specs=placed,
        out_specs=(P("tm", None, "head"), P("tm", None, "head")),
        check_vma=False,
    )
```

```python
import jax
import jax.numpy as jnp
from jax import lax
from jax.experimental import pallas as pl
from jax.experimental.pallas import tpu as pltpu
from jax.sharding import PartitionSpec as P

HEAD_DIM = 64
MEM = 32
TOK = 128
D = 1024
HALF = 512
HEADS = 16
CHIPS = 128
SPLITS = CHIPS // HEADS
OWN = TOK // 2
OWN_MEM = MEM // 2
QROWS = OWN // SPLITS
MEM_PAIRS = OWN_MEM // 2
QUERY_PAIRS = QROWS // 2
PAIRS = MEM_PAIRS + QUERY_PAIRS + 1
STATS_AT = MEM_PAIRS + QUERY_PAIRS
CHUNK_HEADS = 4
GROUP = 2
CHUNK = CHUNK_HEADS * HEAD_DIM
CHUNKS = HEADS // CHUNK_HEADS
LANES = 2 * HEAD_DIM
KEYS = CHIPS * MEM
BLOCK_SEGS = 16
QBLOCK = BLOCK_SEGS * QROWS
KBLOCK = BLOCK_SEGS * MEM
KHALF = KBLOCK // 2
NBLOCKS = CHIPS // BLOCK_SEGS
SCALE = 0.125
MASKED = -3e38
FIRST_VMEM = 60 * 1024 * 1024
MIDDLE_VMEM = 40 * 1024 * 1024
LAST_VMEM = 32 * 1024 * 1024
f32 = jnp.float32
bf16 = jnp.bfloat16


def dot(a, b):
    return jnp.dot(a, b, preferred_element_type=f32)


def dot_nt(a, b):
    return lax.dot_general(a, b, (((1,), (1,)), ((), ())), preferred_element_type=f32)


def dot_tn(a, b):
    return lax.dot_general(a, b, (((0,), (0,)), ((), ())), preferred_element_type=f32)


def three_parts(x):
    high = x.astype(bf16).astype(f32)
    rest = x - high
    middle = rest.astype(bf16).astype(f32)
    low = (rest - middle).astype(bf16).astype(f32)
    return high, middle, low


def low_lanes(shape):
    return lax.broadcasted_iota(jnp.int32, shape, 1) < HEAD_DIM


def split_pair(pair):
    low = low_lanes(pair.shape)
    zero = jnp.zeros_like(pair)
    return jnp.concatenate([jnp.where(low, pair, zero), jnp.where(low, zero, pair)], axis=0)


def head_cols(matrix, head):
    return matrix[:, head * HEAD_DIM : (head + 1) * HEAD_DIM]


def onehot_rows(assign_row, first):
    rows = lax.broadcasted_iota(jnp.int32, (OWN_MEM, TOK), 0) + first
    return (rows == assign_row).astype(f32)


def pre_kernel(
    tok_hbm, asg_hbm, cot_hbm, wq_hbm, wk_hbm, wv_hbm, wo_hbm, msg_hbm, qd_hbm, kv_hbm, side_hbm,
    tok_ref, asg_ref, cot_ref, wq, wk, wv, wo, msg_ref, qd_ref, kv_ref, side_ref, sems, w_sems, out_sems,
):
    half = lax.axis_index("head")
    own_rows = pl.ds(pl.multiple_of(half * OWN, OWN), OWN)
    moves = [(asg_hbm, asg_ref), (tok_hbm, tok_ref), (cot_hbm.at[own_rows, :], cot_ref)]
    copies = [pltpu.make_async_copy(source, target, sems.at[at]) for at, (source, target) in enumerate(moves)]
    weights = []
    for chunk in range(CHUNKS):
        cols = slice(chunk * CHUNK, (chunk + 1) * CHUNK)
        pairs = [
            (wk_hbm.at[:, cols], wk.at[:, cols]),
            (wv_hbm.at[:, cols], wv.at[:, cols]),
            (wq_hbm.at[:, cols], wq.at[:, cols]),
            (wo_hbm.at[cols, :], wo.at[cols, :]),
        ]
        weights.append(
            [pltpu.make_async_copy(source, target, w_sems.at[chunk, at]) for at, (source, target) in enumerate(pairs)]
        )
    for copy in copies + weights[0] + weights[1]:
        copy.start()
    copies[0].wait()
    onehot = onehot_rows(asg_ref[...], half * OWN_MEM)
    counts = jnp.sum(onehot, axis=1, keepdims=True)
    copies[1].wait()
    tokens = tok_ref[...]
    memory = (dot(onehot.astype(bf16), tokens) / counts).astype(bf16)
    rows = jnp.concatenate([memory, tokens], axis=0)
    own_tokens = tok_ref[own_rows, :]
    copies[2].wait()
    own_cotangent = cot_ref[...]
    lane = lax.broadcasted_iota(jnp.int32, (OWN, LANES), 1)
    sublane = lax.broadcasted_iota(jnp.int32, (OWN, LANES), 0)
    sends = []
    for chunk in range(CHUNKS):
        cols = slice(chunk * CHUNK, (chunk + 1) * CHUNK)
        for copy in weights[chunk]:
            copy.wait()
        if chunk + 2 < CHUNKS:
            for copy in weights[chunk + 2]:
                copy.start()
        keys = dot(rows, wk[:, cols]).astype(bf16)
        values = dot(rows, wv[:, cols]).astype(bf16)
        queries = (dot(own_tokens, wq[:, cols]).astype(bf16).astype(f32) * SCALE).astype(bf16)
        grad_out = dot_nt(own_cotangent, wo[cols, :]).astype(bf16)
        for at_head in range(CHUNK_HEADS):
            head = chunk * CHUNK_HEADS + at_head
            pair = jnp.concatenate([head_cols(keys, at_head), head_cols(values, at_head)], axis=1)
            query_pair = jnp.concatenate([head_cols(queries, at_head), head_cols(grad_out, at_head)], axis=1)
            kv_ref[head] = pair[OWN_MEM:]
            qd_ref[head] = query_pair
            mem_pairs = pair[:OWN_MEM].reshape(MEM_PAIRS, 2, LANES)
            msg_ref[:, head, :MEM_PAIRS] = jnp.broadcast_to(mem_pairs[None], (SPLITS, MEM_PAIRS, 2, LANES))
            msg_ref[:, head, MEM_PAIRS:STATS_AT] = query_pair.reshape(SPLITS, QUERY_PAIRS, 2, LANES)
        heads = slice(chunk * CHUNK_HEADS, (chunk + 1) * CHUNK_HEADS)
        sends.append(pltpu.make_async_copy(kv_ref.at[heads], kv_hbm.at[heads], out_sems.at[0, chunk]))
        sends.append(pltpu.make_async_copy(qd_ref.at[heads], qd_hbm.at[heads], out_sems.at[1, chunk]))
        sends[-2].start()
        sends[-1].start()
    for chunk in range(CHUNKS // GROUP):
        group = range(chunk * CHUNK_HEADS * GROUP, (chunk + 1) * CHUNK_HEADS * GROUP)
        query_pairs = [qd_ref[head] for head in group]
        low = low_lanes((OWN, LANES))
        scores = [dot_nt(jnp.where(low, q, jnp.zeros_like(q)), kv_ref[head]) for head, q in zip(group, query_pairs)]
        row_max = [jnp.max(x, axis=1, keepdims=True) for x in scores]
        raised = [jnp.exp(x - m) for x, m in zip(scores, row_max)]
        row_sum = [jnp.sum(x, axis=1, keepdims=True) for x in raised]
        sides = [dot((x / t).astype(bf16), kv_ref[head]) for head, x, t in zip(group, raised, row_sum)]
        for head, query_pair, top, total, side in zip(group, query_pairs, row_max, row_sum, sides):
            log_sum = top + jnp.log(total)
            products = jnp.where(low, 0.0, query_pair.astype(f32) * side)
            delta = jnp.sum(products, axis=1, keepdims=True)
            side_ref[head] = jnp.where(low, log_sum, side)
            stats = jnp.zeros((OWN, LANES), f32)
            for at, part in enumerate(three_parts(log_sum) + three_parts(delta)):
                stats = jnp.where(lane // QROWS == at, part, stats)
            stats = jnp.where(lane % QROWS == sublane % QROWS, stats, 0.0)
            stats = jnp.sum(stats.reshape(SPLITS, QROWS, LANES), axis=1, keepdims=True)
            msg_ref[:, head, STATS_AT] = jnp.broadcast_to(stats, (SPLITS, 2, LANES)).astype(bf16)
        heads = slice(group[0], group[-1] + 1)
        sends.append(pltpu.make_async_copy(msg_ref.at[:, heads], msg_hbm.at[:, heads], out_sems.at[2, chunk]))
        sends.append(pltpu.make_async_copy(side_ref.at[heads], side_hbm.at[heads], out_sems.at[3, chunk]))
        sends[-2].start()
        sends[-1].start()
    for send in sends:
        send.wait()


def attend_kernel(
    msg_ref, away_ref, qd_hbm, own_hbm, side_hbm, tail_ref, mine_ref, other_ref, qd_ref, own_ref, side_ref,
    kv, kvt, scores, dprobs, accum, sems,
):
    moves = [(qd_hbm, qd_ref), (own_hbm, own_ref), (side_hbm, side_ref)]
    copies = [pltpu.make_async_copy(source, target, sems.at[at]) for at, (source, target) in enumerate(moves)]
    for copy in copies:
        copy.start()

    def segs(j):
        return slice(j * BLOCK_SEGS, (j + 1) * BLOCK_SEGS)

    def block(j):
        return slice(j * KBLOCK, (j + 1) * KBLOCK)

    def kv_block(j):
        return kv[block(j), :]

    eye = (
        lax.broadcasted_iota(jnp.int32, (LANES, LANES), 0) == lax.broadcasted_iota(jnp.int32, (LANES, LANES), 1)
    ).astype(bf16)
    visible = lax.broadcasted_iota(jnp.int32, (KBLOCK, QBLOCK), 0) % KHALF // OWN_MEM < (
        lax.broadcasted_iota(jnp.int32, (KBLOCK, QBLOCK), 1) // QROWS
    )

    def fold(op, x):
        return op(x.reshape(KBLOCK // 8, 8, QBLOCK), axis=0)

    row = lax.broadcasted_iota(jnp.int32, (2 * BLOCK_SEGS, QBLOCK), 0)
    column = lax.broadcasted_iota(jnp.int32, (2 * BLOCK_SEGS, QBLOCK), 1)
    spread = (row == column // QROWS * 2).astype(bf16)
    square_row = lax.broadcasted_iota(jnp.int32, (LANES, LANES), 0)
    square_column = lax.broadcasted_iota(jnp.int32, (LANES, LANES), 1)
    same_query = square_row % QROWS == square_column % QROWS
    gather = (
        lax.broadcasted_iota(jnp.int32, (8, LANES), 0) == lax.broadcasted_iota(jnp.int32, (8, LANES), 1) // QROWS
    ).astype(bf16)
    blocks = range(NBLOCKS)
    stats = [dot_tn(spread, msg_ref[segs(i), STATS_AT].reshape(2 * BLOCK_SEGS, LANES)) for i in blocks]
    stats = [dot_nt(gather, jnp.where(same_query, x, 0.0).astype(bf16)) for x in stats]
    state = [
        {"own_log": x[0:1] + x[1:2] + x[2:3], "own_delta": x[3:4] + x[4:5] + x[5:6]} for x in stats
    ]

    def score_stage(i):
        buf, mine = i % 3, state[i]
        kv[i * KBLOCK : i * KBLOCK + KHALF, :] = msg_ref[segs(i), :MEM_PAIRS].reshape(KHALF, LANES)
        kv[i * KBLOCK + KHALF : (i + 1) * KBLOCK, :] = away_ref[segs(i)].reshape(KHALF, LANES)
        kvt[:, block(i)] = dot_nt(eye, kv_block(i)).astype(bf16)
        query_pair = msg_ref[segs(i), MEM_PAIRS:STATS_AT].reshape(QBLOCK, LANES).astype(f32)
        mine["grad_t"] = query_pair.T[HEAD_DIM:]
        mine["pair_rows"] = split_pair(query_pair).astype(bf16)
        top = jnp.full((8, QBLOCK), MASKED, f32)
        for j in range(i + 1):
            both = dot_nt(kv_block(j), mine["pair_rows"])
            score = both[:, :QBLOCK]
            if j == i:
                score = jnp.where(visible, score, MASKED)
            scores[buf, block(j), :] = score
            dprobs[buf, block(j), :] = both[:, QBLOCK:]
            top = jnp.maximum(top, fold(jnp.max, score))
            yield
        mine["row_max"] = jnp.maximum(jnp.max(top, axis=0, keepdims=True), mine["own_log"])

    def middle_stage(i):
        mine = state[i] if i < NBLOCKS else None
        last = state[i - 1] if i > 0 else None
        total = jnp.zeros((8, QBLOCK), f32)
        out = jnp.zeros((LANES, QBLOCK), f32)
        grad = jnp.zeros((LANES, QBLOCK), f32)
        for j in range(min(i + 1, NBLOCKS)):
            right = []
            if mine is not None:
                raised = jnp.exp(scores[i % 3, block(j), :] - mine["row_max"])
                scores[i % 3, block(j), :] = raised
                total = total + fold(jnp.sum, raised)
                right.append(raised.astype(bf16))
            if last is not None and j < i:
                probs = scores[(i - 1) % 3, block(j), :] * last["inverse"]
                dscores = (probs * (dprobs[(i - 1) % 3, block(j), :] - last["delta"])).astype(bf16)
                both = jnp.concatenate([dscores, probs.astype(bf16)], axis=1)
                term = dot(both, last["pair_rows"])
                if j < i - 1:
                    term = accum[block(j), :] + term
                if i < NBLOCKS:
                    accum[block(j), :] = term
                else:
                    mine_ref[j * KHALF : (j + 1) * KHALF, :] = term[:KHALF]
                    other_ref[segs(j)] = term[KHALF:].astype(bf16).reshape(BLOCK_SEGS, MEM_PAIRS, 2, LANES)
                right.append(dscores)
            product = dot(kvt[:, block(j)], jnp.concatenate(right, axis=1) if len(right) > 1 else right[0])
            if mine is not None:
                out = out + product[:, :QBLOCK]
            if last is not None and j < i:
                grad = grad + product[:, -QBLOCK:]
            yield
        if mine is not None:
            own_share = jnp.exp(mine["own_log"] - mine["row_max"])
            row_sum = own_share + jnp.sum(total, axis=0, keepdims=True)
            inverse = 1.0 / row_sum
            out = out[HEAD_DIM:] * inverse
            mine.update(log_sum=mine["row_max"] + jnp.log(row_sum), inverse=inverse, out=out)
            mine["delta"] = (
                jnp.sum(mine["grad_t"] * out, axis=0, keepdims=True) + own_share * inverse * mine["own_delta"]
            )
        if last is not None:
            main = jnp.concatenate([grad[:HEAD_DIM], last["out"]], axis=0).T.astype(bf16)
            tail_ref[segs(i - 1), :QUERY_PAIRS] = main.reshape(BLOCK_SEGS, QUERY_PAIRS, 2, LANES)

    for step in range(NBLOCKS + 2):
        running = []
        if step > 0:
            running.append(middle_stage(step - 1))
        if step < NBLOCKS:
            running.append(score_stage(step))
        while running:
            for one in list(running):
                if next(one, one) is one:
                    running.remove(one)

    stats = [jnp.zeros((LANES, LANES), f32) for _ in blocks]
    for at in range(3):
        parts = [three_parts(one["log_sum"])[at] for one in state]
        stats = [jnp.where(square_row // QROWS == at, part, x) for part, x in zip(parts, stats)]
    stats = [dot_nt(spread, jnp.where(same_query, x, 0.0).astype(bf16)) for x in stats]
    for i in blocks:
        tail_ref[segs(i), QUERY_PAIRS] = stats[i].astype(bf16).reshape(BLOCK_SEGS, 2, LANES)
    for copy in copies:
        copy.wait()


def join_kernel(mine_ref, other_ref, tail_ref, out_ref):
    out_ref[:, MEM_PAIRS:] = tail_ref[...]
    for j in range(NBLOCKS):
        segs = slice(j * BLOCK_SEGS, (j + 1) * BLOCK_SEGS)
        far = other_ref[segs].reshape(KHALF, LANES).astype(f32)
        total = (mine_ref[j * KHALF : (j + 1) * KHALF, :] + far).astype(bf16)
        out_ref[segs, :MEM_PAIRS] = total.reshape(BLOCK_SEGS, MEM_PAIRS, 2, LANES)


def post_kernel(
    msg_ref, asg_ref, qd_ref, kv_ref, side_ref, wq, wk, wv, wo, out_ref, mine_ref, other_ref,
):
    half = lax.axis_index("head")
    offset = pl.multiple_of(half * HALF, HALF)
    away = pl.multiple_of((1 - half) * HALF, HALF)
    onehot = onehot_rows(asg_ref[...], half * OWN_MEM)
    counts = jnp.sum(onehot, axis=1, keepdims=True)
    onehot = onehot.astype(bf16)
    heads = range(HEADS)
    def mem_sum(head):
        parts = [msg_ref[k, head, :MEM_PAIRS].reshape(OWN_MEM, LANES).astype(f32) for k in range(SPLITS)]
        return sum(parts[1:], parts[0])

    mem_pairs = [mem_sum(head) for head in heads]
    pair_rows = [split_pair(qd_ref[head]) for head in heads]
    both = [dot_nt(pair_rows[head], kv_ref[head]) for head in heads]
    returned = [msg_ref[:, head, MEM_PAIRS:STATS_AT].reshape(OWN, LANES).astype(f32) for head in heads]
    sublane = lax.broadcasted_iota(jnp.int32, (OWN, LANES), 0)
    lane = lax.broadcasted_iota(jnp.int32, (OWN, LANES), 1)
    same_query = sublane % QROWS == lane % QROWS

    def log_sum_of(head):
        stats = msg_ref[:, head, STATS_AT].astype(f32)[:, :1]
        stats = jnp.broadcast_to(stats, (SPLITS, QROWS, LANES)).reshape(OWN, LANES)
        return jnp.sum(jnp.where(same_query, stats, 0.0), axis=1, keepdims=True)

    log_sums = [log_sum_of(head) for head in heads]
    shares = [jnp.exp(side_ref[head][:, :1] - log_sums[head]) for head in heads]
    mains = [(returned[head] + shares[head] * side_ref[head]).astype(bf16).astype(f32) for head in heads]
    products = [qd_ref[head].astype(f32) * mains[head] for head in heads]
    deltas = [jnp.sum(jnp.where(low_lanes(x.shape), 0.0, x), axis=1, keepdims=True) for x in products]
    probs = [jnp.exp(both[head][:OWN] - log_sums[head]) for head in heads]
    dscores = [(probs[head] * (both[head][OWN:] - deltas[head])).astype(bf16) for head in heads]
    own_grads = [dot(dscores[head], kv_ref[head]) for head in heads]
    own_pairs = [
        dot_tn(jnp.concatenate([dscores[head], probs[head].astype(bf16)], axis=0), pair_rows[head]) for head in heads
    ]
    grads = [jnp.concatenate([own_pairs[head], mem_pairs[head]], axis=0) for head in heads]
    heads_out = [x[:, HEAD_DIM:] for x in mains]
    query_grads = [((returned[head] + own_grads[head]) * SCALE)[:, :HEAD_DIM] for head in heads]
    key_grads = [x[:, :HEAD_DIM] for x in grads]
    value_grads = [x[:, HEAD_DIM:] for x in grads]

    def merge(parts):
        return jnp.concatenate(parts, axis=1).astype(bf16)

    heads_out = merge(heads_out)
    query_grads = merge(query_grads)
    key_grads = merge(key_grads)
    value_grads = merge(value_grads)
    own_rows = pl.ds(pl.multiple_of(half * OWN, OWN), OWN)
    for start, keep in ((away, False), (offset, True)):
        rows = pl.ds(start, HALF)
        total = dot_nt(key_grads, wk[rows, :]) + dot_nt(value_grads, wv[rows, :])
        high, middle, low = three_parts(total[TOK:] / counts)
        spread = dot_tn(onehot, high.astype(bf16)) + dot_tn(onehot, middle.astype(bf16)) + dot_tn(onehot, low.astype(bf16))
        grad_rows = pl.ds(0, TOK)
        if keep:
            mine_ref[...] = total[:TOK] + spread
            mine_ref[own_rows, :] += dot_nt(query_grads, wq[rows, :])
        else:
            other_ref[grad_rows, :] = total[:TOK] + spread
            other_ref[own_rows, :] += dot_nt(query_grads, wq[rows, :])
    other_ref[TOK:, :] = dot(heads_out, wo[:, pl.ds(away, HALF)])
    out_ref[...] = dot(heads_out, wo[:, pl.ds(offset, HALF)])


def finish_kernel(attended_ref, mine_ref, arrived_ref, out_ref, grad_ref):
    half = lax.axis_index("head")
    own_rows = pl.ds(pl.multiple_of(half * OWN, OWN), OWN)
    far_rows = pl.ds(pl.multiple_of((1 - half) * OWN, OWN), OWN)
    out_ref[0, own_rows, :] = attended_ref[...].astype(bf16)
    out_ref[0, far_rows, :] = arrived_ref[TOK:, :].astype(bf16)
    grad_ref[0] = (mine_ref[...] + arrived_ref[:TOK, :]).astype(bf16)


def params(vmem_bytes):
    return pltpu.CompilerParams(vmem_limit_bytes=vmem_bytes)


def vmem():
    return pl.BlockSpec(memory_space=pltpu.VMEM)


def hbm():
    return pl.BlockSpec(memory_space=pltpu.HBM)


def anywhere():
    return pl.BlockSpec(memory_space=pl.ANY)


def swap_cores(x):
    return lax.ppermute(x, "head", [(0, 1), (1, 0)])


def shards(video, assign, w_query, w_key, w_value, w_out, cotangent):
    message_shape = (SPLITS, HEADS, PAIRS, 2, LANES)
    chip_shape = (CHIPS, PAIRS, 2, LANES)
    message, query_pairs, own_pairs, own_sides = pl.pallas_call(
        pre_kernel,
        out_shape=(
            jax.ShapeDtypeStruct(message_shape, bf16),
            jax.ShapeDtypeStruct((HEADS, OWN, LANES), bf16),
            jax.ShapeDtypeStruct((HEADS, TOK, LANES), bf16),
            jax.ShapeDtypeStruct((HEADS, OWN, LANES), f32),
        ),
        in_specs=[anywhere()] * 7,
        out_specs=(hbm(), hbm(), hbm(), hbm()),
        scratch_shapes=[
            pltpu.VMEM((TOK, D), bf16),
            pltpu.VMEM((1, TOK), jnp.int32),
            pltpu.VMEM((OWN, D), bf16),
            *[pltpu.VMEM((D, D), bf16)] * 4,
            pltpu.VMEM(message_shape, bf16),
            pltpu.VMEM((HEADS, OWN, LANES), bf16),
            pltpu.VMEM((HEADS, TOK, LANES), bf16),
            pltpu.VMEM((HEADS, OWN, LANES), f32),
            pltpu.SemaphoreType.DMA((3,)),
            pltpu.SemaphoreType.DMA((CHUNKS, 4)),
            pltpu.SemaphoreType.DMA((4, CHUNKS)),
        ],
        compiler_params=params(FIRST_VMEM),
        name="project",
    )(video[0], assign, cotangent[0], w_query, w_key, w_value, w_out)

    received = lax.all_to_all(message.reshape(chip_shape), "tm", 0, 0, tiled=True)
    away = swap_cores(received[:, :MEM_PAIRS])
    part_shape = (CHIPS, MEM_PAIRS, 2, LANES)
    tail_shape = (CHIPS, PAIRS - MEM_PAIRS, 2, LANES)
    mine_shape = (CHIPS * OWN_MEM, LANES)
    saved = (query_pairs, own_pairs, own_sides)
    tail, mine, other, *saved = pl.pallas_call(
        attend_kernel,
        out_shape=(
            jax.ShapeDtypeStruct(tail_shape, bf16),
            jax.ShapeDtypeStruct(mine_shape, f32),
            jax.ShapeDtypeStruct(part_shape, bf16),
            *[jax.ShapeDtypeStruct(one.shape, one.dtype) for one in saved],
        ),
        in_specs=[vmem(), vmem()] + [anywhere()] * 3,
        out_specs=(vmem(),) * 6,
        scratch_shapes=[
            pltpu.VMEM((KEYS, LANES), bf16),
            pltpu.VMEM((LANES, KEYS), bf16),
            pltpu.VMEM((3, KEYS, QBLOCK), f32),
            pltpu.VMEM((3, KEYS, QBLOCK), f32),
            pltpu.VMEM((KEYS, LANES), f32),
            pltpu.SemaphoreType.DMA((3,)),
        ],
        compiler_params=params(MIDDLE_VMEM),
        name="attend",
    )(received, away, *saved)
    answer = pl.pallas_call(
        join_kernel,
        out_shape=jax.ShapeDtypeStruct(chip_shape, bf16),
        in_specs=[vmem()] * 3,
        out_specs=vmem(),
        compiler_params=params(LAST_VMEM),
        name="join",
    )(mine, swap_cores(other), tail)
    returned = lax.all_to_all(answer, "tm", 0, 0, tiled=True).reshape(message_shape)

    attended, mine, other = pl.pallas_call(
        post_kernel,
        out_shape=(
            jax.ShapeDtypeStruct((OWN, HALF), f32),
            jax.ShapeDtypeStruct((TOK, HALF), f32),
            jax.ShapeDtypeStruct((TOK + OWN, HALF), f32),
        ),
        in_specs=[vmem()] * 9,
        out_specs=(vmem(), vmem(), vmem()),
        compiler_params=params(LAST_VMEM),
        name="gradients",
    )(returned, assign, *saved, w_query, w_key, w_value, w_out)
    half_shape = jax.ShapeDtypeStruct((1, TOK, HALF), bf16)
    return pl.pallas_call(
        finish_kernel,
        out_shape=(half_shape, half_shape),
        in_specs=[vmem()] * 3,
        out_specs=(vmem(), vmem()),
        compiler_params=params(LAST_VMEM),
        name="finish",
    )(attended, mine, swap_cores(other))


def solution(mesh):
    placed = (P("tm", None, None), P("tm", None), P(), P(), P(), P(), P("tm", None, None))
    return jax.shard_map(
        shards,
        mesh=mesh,
        in_specs=placed,
        out_specs=(P("tm", None, "head"), P("tm", None, "head")),
        check_vma=False,
    )
```

```python
import jax
import jax.numpy as jnp
from jax import lax
from jax.experimental import pallas as pl
from jax.experimental.pallas import tpu as pltpu
from jax.sharding import PartitionSpec as P

HEAD_DIM = 64
MEM = 32
TOK = 128
D = 1024
HALF = 512
HEADS = 16
CHIPS = 128
SPLITS = CHIPS // HEADS
OWN = TOK // 2
OWN_MEM = MEM // 2
QROWS = OWN // SPLITS
MEM_PAIRS = OWN_MEM // 2
QUERY_PAIRS = QROWS // 2
PAIRS = MEM_PAIRS + QUERY_PAIRS + 1
STATS_AT = MEM_PAIRS + QUERY_PAIRS
CHUNK_HEADS = 4
GROUP = 2
CHUNK = CHUNK_HEADS * HEAD_DIM
CHUNKS = HEADS // CHUNK_HEADS
LANES = 2 * HEAD_DIM
KEYS = CHIPS * MEM
BLOCK_SEGS = 16
QBLOCK = BLOCK_SEGS * QROWS
KBLOCK = BLOCK_SEGS * MEM
KHALF = KBLOCK // 2
NBLOCKS = CHIPS // BLOCK_SEGS
SCALE = 0.125
MASKED = -3e38
FIRST_VMEM = 60 * 1024 * 1024
MIDDLE_VMEM = 40 * 1024 * 1024
LAST_VMEM = 32 * 1024 * 1024
f32 = jnp.float32
bf16 = jnp.bfloat16


def dot(a, b):
    return jnp.dot(a, b, preferred_element_type=f32)


def dot_nt(a, b):
    return lax.dot_general(a, b, (((1,), (1,)), ((), ())), preferred_element_type=f32)


def dot_tn(a, b):
    return lax.dot_general(a, b, (((0,), (0,)), ((), ())), preferred_element_type=f32)


def three_parts(x):
    high = x.astype(bf16).astype(f32)
    rest = x - high
    middle = rest.astype(bf16).astype(f32)
    low = (rest - middle).astype(bf16).astype(f32)
    return high, middle, low


def low_lanes(shape):
    return lax.broadcasted_iota(jnp.int32, shape, 1) < HEAD_DIM


def split_pair(pair):
    low = low_lanes(pair.shape)
    zero = jnp.zeros_like(pair)
    return jnp.concatenate([jnp.where(low, pair, zero), jnp.where(low, zero, pair)], axis=0)


def head_cols(matrix, head):
    return matrix[:, head * HEAD_DIM : (head + 1) * HEAD_DIM]


def onehot_rows(assign_row, first):
    rows = lax.broadcasted_iota(jnp.int32, (OWN_MEM, TOK), 0) + first
    return (rows == assign_row).astype(f32)


def pre_kernel(
    tok_hbm, asg_hbm, cot_hbm, wq_hbm, wk_hbm, wv_hbm, wo_hbm, msg_hbm, qd_hbm, kv_hbm, side_hbm,
    tok_ref, asg_ref, cot_ref, wq, wk, wv, wo, msg_ref, qd_ref, kv_ref, side_ref, sems, w_sems, out_sems,
):
    half = lax.axis_index("head")
    own_rows = pl.ds(pl.multiple_of(half * OWN, OWN), OWN)
    moves = [(asg_hbm, asg_ref), (tok_hbm, tok_ref), (cot_hbm.at[own_rows, :], cot_ref)]
    copies = [pltpu.make_async_copy(source, target, sems.at[at]) for at, (source, target) in enumerate(moves)]
    weights = []
    for chunk in range(CHUNKS):
        cols = slice(chunk * CHUNK, (chunk + 1) * CHUNK)
        pairs = [
            (wk_hbm.at[:, cols], wk.at[:, cols]),
            (wv_hbm.at[:, cols], wv.at[:, cols]),
            (wq_hbm.at[:, cols], wq.at[:, cols]),
            (wo_hbm.at[cols, :], wo.at[cols, :]),
        ]
        weights.append(
            [pltpu.make_async_copy(source, target, w_sems.at[chunk, at]) for at, (source, target) in enumerate(pairs)]
        )
    for copy in copies + weights[0] + weights[1]:
        copy.start()
    copies[0].wait()
    onehot = onehot_rows(asg_ref[...], half * OWN_MEM)
    counts = jnp.sum(onehot, axis=1, keepdims=True)
    copies[1].wait()
    tokens = tok_ref[...]
    memory = (dot(onehot.astype(bf16), tokens) / counts).astype(bf16)
    rows = jnp.concatenate([memory, tokens], axis=0)
    own_tokens = tok_ref[own_rows, :]
    copies[2].wait()
    own_cotangent = cot_ref[...]
    lane = lax.broadcasted_iota(jnp.int32, (OWN, LANES), 1)
    sublane = lax.broadcasted_iota(jnp.int32, (OWN, LANES), 0)
    sends = []
    for chunk in range(CHUNKS):
        cols = slice(chunk * CHUNK, (chunk + 1) * CHUNK)
        for copy in weights[chunk]:
            copy.wait()
        if chunk + 2 < CHUNKS:
            for copy in weights[chunk + 2]:
                copy.start()
        keys = dot(rows, wk[:, cols]).astype(bf16)
        values = dot(rows, wv[:, cols]).astype(bf16)
        queries = (dot(own_tokens, wq[:, cols]).astype(bf16).astype(f32) * SCALE).astype(bf16)
        grad_out = dot_nt(own_cotangent, wo[cols, :]).astype(bf16)
        for at_head in range(CHUNK_HEADS):
            head = chunk * CHUNK_HEADS + at_head
            pair = jnp.concatenate([head_cols(keys, at_head), head_cols(values, at_head)], axis=1)
            query_pair = jnp.concatenate([head_cols(queries, at_head), head_cols(grad_out, at_head)], axis=1)
            kv_ref[head] = pair[OWN_MEM:]
            qd_ref[head] = query_pair
            mem_pairs = pair[:OWN_MEM].reshape(MEM_PAIRS, 2, LANES)
            msg_ref[:, head, :MEM_PAIRS] = jnp.broadcast_to(mem_pairs[None], (SPLITS, MEM_PAIRS, 2, LANES))
            msg_ref[:, head, MEM_PAIRS:STATS_AT] = query_pair.reshape(SPLITS, QUERY_PAIRS, 2, LANES)
        heads = slice(chunk * CHUNK_HEADS, (chunk + 1) * CHUNK_HEADS)
        sends.append(pltpu.make_async_copy(kv_ref.at[heads], kv_hbm.at[heads], out_sems.at[0, chunk]))
        sends.append(pltpu.make_async_copy(qd_ref.at[heads], qd_hbm.at[heads], out_sems.at[1, chunk]))
        sends[-2].start()
        sends[-1].start()
    for chunk in range(CHUNKS // GROUP):
        group = range(chunk * CHUNK_HEADS * GROUP, (chunk + 1) * CHUNK_HEADS * GROUP)
        query_pairs = [qd_ref[head] for head in group]
        low = low_lanes((OWN, LANES))
        scores = [dot_nt(jnp.where(low, q, jnp.zeros_like(q)), kv_ref[head]) for head, q in zip(group, query_pairs)]
        row_max = [jnp.max(x, axis=1, keepdims=True) for x in scores]
        raised = [jnp.exp(x - m) for x, m in zip(scores, row_max)]
        row_sum = [jnp.sum(x, axis=1, keepdims=True) for x in raised]
        sides = [dot((x / t).astype(bf16), kv_ref[head]) for head, x, t in zip(group, raised, row_sum)]
        for head, query_pair, top, total, side in zip(group, query_pairs, row_max, row_sum, sides):
            products = jnp.where(low, 0.0, query_pair.astype(f32) * side)
            delta = jnp.sum(products, axis=1, keepdims=True)
            side_ref[head] = jnp.where(lane == 0, top, jnp.where(low, total, side))
            stats = jnp.zeros((OWN, LANES), f32)
            for at, part in enumerate(three_parts(top) + three_parts(total) + three_parts(delta)):
                stats = jnp.where(lane // QROWS == at, part, stats)
            stats = jnp.where(lane % QROWS == sublane % QROWS, stats, 0.0)
            stats = jnp.sum(stats.reshape(SPLITS, QROWS, LANES), axis=1, keepdims=True)
            msg_ref[:, head, STATS_AT] = jnp.broadcast_to(stats, (SPLITS, 2, LANES)).astype(bf16)
        heads = slice(group[0], group[-1] + 1)
        sends.append(pltpu.make_async_copy(msg_ref.at[:, heads], msg_hbm.at[:, heads], out_sems.at[2, chunk]))
        sends.append(pltpu.make_async_copy(side_ref.at[heads], side_hbm.at[heads], out_sems.at[3, chunk]))
        sends[-2].start()
        sends[-1].start()
    for send in sends:
        send.wait()


def attend_kernel(
    msg_ref, away_ref, qd_hbm, own_hbm, side_hbm, tail_ref, mine_ref, other_ref, qd_ref, own_ref, side_ref,
    kv, kvt, scores, dprobs, accum, sems,
):
    moves = [(qd_hbm, qd_ref), (own_hbm, own_ref), (side_hbm, side_ref)]
    copies = [pltpu.make_async_copy(source, target, sems.at[at]) for at, (source, target) in enumerate(moves)]
    for copy in copies:
        copy.start()

    def segs(j):
        return slice(j * BLOCK_SEGS, (j + 1) * BLOCK_SEGS)

    def block(j):
        return slice(j * KBLOCK, (j + 1) * KBLOCK)

    def kv_block(j):
        return kv[block(j), :]

    eye = (
        lax.broadcasted_iota(jnp.int32, (LANES, LANES), 0) == lax.broadcasted_iota(jnp.int32, (LANES, LANES), 1)
    ).astype(bf16)
    visible = lax.broadcasted_iota(jnp.int32, (KBLOCK, QBLOCK), 0) % KHALF // OWN_MEM < (
        lax.broadcasted_iota(jnp.int32, (KBLOCK, QBLOCK), 1) // QROWS
    )

    def fold(op, x):
        return op(x.reshape(KBLOCK // 8, 8, QBLOCK), axis=0)

    row = lax.broadcasted_iota(jnp.int32, (2 * BLOCK_SEGS, QBLOCK), 0)
    column = lax.broadcasted_iota(jnp.int32, (2 * BLOCK_SEGS, QBLOCK), 1)
    spread = (row == column // QROWS * 2).astype(bf16)
    square_row = lax.broadcasted_iota(jnp.int32, (LANES, LANES), 0)
    square_column = lax.broadcasted_iota(jnp.int32, (LANES, LANES), 1)
    same_query = square_row % QROWS == square_column % QROWS
    gather = (
        lax.broadcasted_iota(jnp.int32, (16, LANES), 0) == lax.broadcasted_iota(jnp.int32, (16, LANES), 1) // QROWS
    ).astype(bf16)
    blocks = range(NBLOCKS)
    stats = [dot_tn(spread, msg_ref[segs(i), STATS_AT].reshape(2 * BLOCK_SEGS, LANES)) for i in blocks]
    stats = [dot_nt(gather, jnp.where(same_query, x, 0.0).astype(bf16)) for x in stats]
    state = [
        {
            "own_max": x[0:1] + x[1:2] + x[2:3],
            "own_sum": x[3:4] + x[4:5] + x[5:6],
            "own_delta": x[6:7] + x[7:8] + x[8:9],
        }
        for x in stats
    ]

    def score_stage(i):
        buf, mine = i % 3, state[i]
        kv[i * KBLOCK : i * KBLOCK + KHALF, :] = msg_ref[segs(i), :MEM_PAIRS].reshape(KHALF, LANES)
        kv[i * KBLOCK + KHALF : (i + 1) * KBLOCK, :] = away_ref[segs(i)].reshape(KHALF, LANES)
        kvt[:, block(i)] = dot_nt(eye, kv_block(i)).astype(bf16)
        query_pair = msg_ref[segs(i), MEM_PAIRS:STATS_AT].reshape(QBLOCK, LANES).astype(f32)
        mine["grad_t"] = query_pair.T[HEAD_DIM:]
        mine["pair_rows"] = split_pair(query_pair).astype(bf16)
        top = jnp.full((8, QBLOCK), MASKED, f32)
        for j in range(i + 1):
            both = dot_nt(kv_block(j), mine["pair_rows"])
            score = both[:, :QBLOCK]
            if j == i:
                score = jnp.where(visible, score, MASKED)
            scores[buf, block(j), :] = score
            dprobs[buf, block(j), :] = both[:, QBLOCK:]
            top = jnp.maximum(top, fold(jnp.max, score))
            yield
        mine["row_max"] = jnp.maximum(jnp.max(top, axis=0, keepdims=True), mine["own_max"])

    def middle_stage(i):
        mine = state[i] if i < NBLOCKS else None
        last = state[i - 1] if i > 0 else None
        total = jnp.zeros((8, QBLOCK), f32)
        out = jnp.zeros((LANES, QBLOCK), f32)
        grad = jnp.zeros((LANES, QBLOCK), f32)
        for j in range(min(i + 1, NBLOCKS)):
            right = []
            if mine is not None:
                raised = jnp.exp(scores[i % 3, block(j), :] - mine["row_max"])
                scores[i % 3, block(j), :] = raised
                total = total + fold(jnp.sum, raised)
                right.append(raised.astype(bf16))
            if last is not None and j < i:
                probs = scores[(i - 1) % 3, block(j), :] * last["inverse"]
                dscores = (probs * (dprobs[(i - 1) % 3, block(j), :] - last["delta"])).astype(bf16)
                both = jnp.concatenate([dscores, probs.astype(bf16)], axis=1)
                term = dot(both, last["pair_rows"])
                if j < i - 1:
                    term = accum[block(j), :] + term
                if i < NBLOCKS:
                    accum[block(j), :] = term
                else:
                    mine_ref[j * KHALF : (j + 1) * KHALF, :] = term[:KHALF]
                    other_ref[segs(j)] = term[KHALF:].astype(bf16).reshape(BLOCK_SEGS, MEM_PAIRS, 2, LANES)
                right.append(dscores)
            product = dot(kvt[:, block(j)], jnp.concatenate(right, axis=1) if len(right) > 1 else right[0])
            if mine is not None:
                out = out + product[:, :QBLOCK]
            if last is not None and j < i:
                grad = grad + product[:, -QBLOCK:]
            yield
        if mine is not None:
            own_share = mine["own_sum"] * jnp.exp(mine["own_max"] - mine["row_max"])
            row_sum = own_share + jnp.sum(total, axis=0, keepdims=True)
            inverse = 1.0 / row_sum
            out = out[HEAD_DIM:] * inverse
            mine.update(row_sum=row_sum, inverse=inverse, out=out)
            mine["delta"] = (
                jnp.sum(mine["grad_t"] * out, axis=0, keepdims=True) + own_share * inverse * mine["own_delta"]
            )
        if last is not None:
            main = jnp.concatenate([grad[:HEAD_DIM], last["out"]], axis=0).T.astype(bf16)
            tail_ref[segs(i - 1), :QUERY_PAIRS] = main.reshape(BLOCK_SEGS, QUERY_PAIRS, 2, LANES)

    for step in range(NBLOCKS + 2):
        running = []
        if step > 0:
            running.append(middle_stage(step - 1))
        if step < NBLOCKS:
            running.append(score_stage(step))
        while running:
            for one in list(running):
                if next(one, one) is one:
                    running.remove(one)

    stats = [jnp.zeros((LANES, LANES), f32) for _ in blocks]
    sent = [three_parts(one["row_max"]) + three_parts(one["row_sum"]) for one in state]
    for at in range(6):
        parts = [one[at] for one in sent]
        stats = [jnp.where(square_row // QROWS == at, part, x) for part, x in zip(parts, stats)]
    stats = [dot_nt(spread, jnp.where(same_query, x, 0.0).astype(bf16)) for x in stats]
    for i in blocks:
        tail_ref[segs(i), QUERY_PAIRS] = stats[i].astype(bf16).reshape(BLOCK_SEGS, 2, LANES)
    for copy in copies:
        copy.wait()


def join_kernel(mine_ref, other_ref, tail_ref, out_ref):
    out_ref[:, MEM_PAIRS:] = tail_ref[...]
    for j in range(NBLOCKS):
        segs = slice(j * BLOCK_SEGS, (j + 1) * BLOCK_SEGS)
        far = other_ref[segs].reshape(KHALF, LANES).astype(f32)
        total = (mine_ref[j * KHALF : (j + 1) * KHALF, :] + far).astype(bf16)
        out_ref[segs, :MEM_PAIRS] = total.reshape(BLOCK_SEGS, MEM_PAIRS, 2, LANES)


def post_kernel(
    msg_ref, asg_ref, qd_ref, kv_ref, side_ref, wq, wk, wv, wo, out_ref, mine_ref, other_ref,
):
    half = lax.axis_index("head")
    offset = pl.multiple_of(half * HALF, HALF)
    away = pl.multiple_of((1 - half) * HALF, HALF)
    onehot = onehot_rows(asg_ref[...], half * OWN_MEM)
    counts = jnp.sum(onehot, axis=1, keepdims=True)
    onehot = onehot.astype(bf16)
    heads = range(HEADS)
    def mem_sum(head):
        parts = [msg_ref[k, head, :MEM_PAIRS].reshape(OWN_MEM, LANES).astype(f32) for k in range(SPLITS)]
        return sum(parts[1:], parts[0])

    mem_pairs = [mem_sum(head) for head in heads]
    pair_rows = [split_pair(qd_ref[head]) for head in heads]
    both = [dot_nt(pair_rows[head], kv_ref[head]) for head in heads]
    returned = [msg_ref[:, head, MEM_PAIRS:STATS_AT].reshape(OWN, LANES).astype(f32) for head in heads]
    sublane = lax.broadcasted_iota(jnp.int32, (OWN, LANES), 0)
    lane = lax.broadcasted_iota(jnp.int32, (OWN, LANES), 1)
    same_query = sublane % QROWS == lane % QROWS

    part = lax.broadcasted_iota(jnp.int32, (LANES, 2 * LANES), 0) // QROWS
    wanted = lax.broadcasted_iota(jnp.int32, (LANES, 2 * LANES), 1) // LANES
    pick = (part // 3 == wanted).astype(bf16)

    def stats_of(head):
        stats = msg_ref[:, head, STATS_AT].astype(f32)[:, :1]
        stats = jnp.broadcast_to(stats, (SPLITS, QROWS, LANES)).reshape(OWN, LANES)
        return dot(jnp.where(same_query, stats, 0.0).astype(bf16), pick)

    stats = [stats_of(head) for head in heads]
    row_max = [x[:, :LANES] for x in stats]
    inverse = [1.0 / x[:, LANES:] for x in stats]
    shares = [
        side_ref[head][:, 1:2] * jnp.exp(side_ref[head][:, :1] - row_max[head]) * inverse[head] for head in heads
    ]
    mains = [(returned[head] + shares[head] * side_ref[head]).astype(bf16).astype(f32) for head in heads]
    products = [qd_ref[head].astype(f32) * mains[head] for head in heads]
    deltas = [jnp.sum(jnp.where(low_lanes(x.shape), 0.0, x), axis=1, keepdims=True) for x in products]
    probs = [jnp.exp(both[head][:OWN] - row_max[head]) * inverse[head] for head in heads]
    dscores = [(probs[head] * (both[head][OWN:] - deltas[head])).astype(bf16) for head in heads]
    own_grads = [dot(dscores[head], kv_ref[head]) for head in heads]
    own_pairs = [
        dot_tn(jnp.concatenate([dscores[head], probs[head].astype(bf16)], axis=0), pair_rows[head]) for head in heads
    ]
    grads = [jnp.concatenate([own_pairs[head], mem_pairs[head]], axis=0) for head in heads]
    heads_out = [x[:, HEAD_DIM:] for x in mains]
    query_grads = [((returned[head] + own_grads[head]) * SCALE)[:, :HEAD_DIM] for head in heads]
    key_grads = [x[:, :HEAD_DIM] for x in grads]
    value_grads = [x[:, HEAD_DIM:] for x in grads]

    def merge(parts):
        return jnp.concatenate(parts, axis=1).astype(bf16)

    heads_out = merge(heads_out)
    query_grads = merge(query_grads)
    key_grads = merge(key_grads)
    value_grads = merge(value_grads)
    own_rows = pl.ds(pl.multiple_of(half * OWN, OWN), OWN)
    for start, keep in ((away, False), (offset, True)):
        rows = pl.ds(start, HALF)
        total = dot_nt(key_grads, wk[rows, :]) + dot_nt(value_grads, wv[rows, :])
        high, middle, low = three_parts(total[TOK:] / counts)
        spread = dot_tn(onehot, high.astype(bf16)) + dot_tn(onehot, middle.astype(bf16)) + dot_tn(onehot, low.astype(bf16))
        grad_rows = pl.ds(0, TOK)
        if keep:
            mine_ref[...] = total[:TOK] + spread
            mine_ref[own_rows, :] += dot_nt(query_grads, wq[rows, :])
        else:
            other_ref[grad_rows, :] = total[:TOK] + spread
            other_ref[own_rows, :] += dot_nt(query_grads, wq[rows, :])
    other_ref[TOK:, :] = dot(heads_out, wo[:, pl.ds(away, HALF)])
    out_ref[...] = dot(heads_out, wo[:, pl.ds(offset, HALF)])


def finish_kernel(attended_ref, mine_ref, arrived_ref, out_ref, grad_ref):
    half = lax.axis_index("head")
    own_rows = pl.ds(pl.multiple_of(half * OWN, OWN), OWN)
    far_rows = pl.ds(pl.multiple_of((1 - half) * OWN, OWN), OWN)
    out_ref[0, own_rows, :] = attended_ref[...].astype(bf16)
    out_ref[0, far_rows, :] = arrived_ref[TOK:, :].astype(bf16)
    grad_ref[0] = (mine_ref[...] + arrived_ref[:TOK, :]).astype(bf16)


def params(vmem_bytes):
    return pltpu.CompilerParams(vmem_limit_bytes=vmem_bytes)


def vmem():
    return pl.BlockSpec(memory_space=pltpu.VMEM)


def hbm():
    return pl.BlockSpec(memory_space=pltpu.HBM)


def anywhere():
    return pl.BlockSpec(memory_space=pl.ANY)


def swap_cores(x):
    return lax.ppermute(x, "head", [(0, 1), (1, 0)])


def shards(video, assign, w_query, w_key, w_value, w_out, cotangent):
    message_shape = (SPLITS, HEADS, PAIRS, 2, LANES)
    chip_shape = (CHIPS, PAIRS, 2, LANES)
    message, query_pairs, own_pairs, own_sides = pl.pallas_call(
        pre_kernel,
        out_shape=(
            jax.ShapeDtypeStruct(message_shape, bf16),
            jax.ShapeDtypeStruct((HEADS, OWN, LANES), bf16),
            jax.ShapeDtypeStruct((HEADS, TOK, LANES), bf16),
            jax.ShapeDtypeStruct((HEADS, OWN, LANES), f32),
        ),
        in_specs=[anywhere()] * 7,
        out_specs=(hbm(), hbm(), hbm(), hbm()),
        scratch_shapes=[
            pltpu.VMEM((TOK, D), bf16),
            pltpu.VMEM((1, TOK), jnp.int32),
            pltpu.VMEM((OWN, D), bf16),
            *[pltpu.VMEM((D, D), bf16)] * 4,
            pltpu.VMEM(message_shape, bf16),
            pltpu.VMEM((HEADS, OWN, LANES), bf16),
            pltpu.VMEM((HEADS, TOK, LANES), bf16),
            pltpu.VMEM((HEADS, OWN, LANES), f32),
            pltpu.SemaphoreType.DMA((3,)),
            pltpu.SemaphoreType.DMA((CHUNKS, 4)),
            pltpu.SemaphoreType.DMA((4, CHUNKS)),
        ],
        compiler_params=params(FIRST_VMEM),
        name="project",
    )(video[0], assign, cotangent[0], w_query, w_key, w_value, w_out)

    received = lax.all_to_all(message.reshape(chip_shape), "tm", 0, 0, tiled=True)
    away = swap_cores(received[:, :MEM_PAIRS])
    part_shape = (CHIPS, MEM_PAIRS, 2, LANES)
    tail_shape = (CHIPS, PAIRS - MEM_PAIRS, 2, LANES)
    mine_shape = (CHIPS * OWN_MEM, LANES)
    saved = (query_pairs, own_pairs, own_sides)
    tail, mine, other, *saved = pl.pallas_call(
        attend_kernel,
        out_shape=(
            jax.ShapeDtypeStruct(tail_shape, bf16),
            jax.ShapeDtypeStruct(mine_shape, f32),
            jax.ShapeDtypeStruct(part_shape, bf16),
            *[jax.ShapeDtypeStruct(one.shape, one.dtype) for one in saved],
        ),
        in_specs=[vmem(), vmem()] + [anywhere()] * 3,
        out_specs=(vmem(),) * 6,
        scratch_shapes=[
            pltpu.VMEM((KEYS, LANES), bf16),
            pltpu.VMEM((LANES, KEYS), bf16),
            pltpu.VMEM((3, KEYS, QBLOCK), f32),
            pltpu.VMEM((3, KEYS, QBLOCK), f32),
            pltpu.VMEM((KEYS, LANES), f32),
            pltpu.SemaphoreType.DMA((3,)),
        ],
        compiler_params=params(MIDDLE_VMEM),
        name="attend",
    )(received, away, *saved)
    answer = pl.pallas_call(
        join_kernel,
        out_shape=jax.ShapeDtypeStruct(chip_shape, bf16),
        in_specs=[vmem()] * 3,
        out_specs=vmem(),
        compiler_params=params(LAST_VMEM),
        name="join",
    )(mine, swap_cores(other), tail)
    returned = lax.all_to_all(answer, "tm", 0, 0, tiled=True).reshape(message_shape)

    attended, mine, other = pl.pallas_call(
        post_kernel,
        out_shape=(
            jax.ShapeDtypeStruct((OWN, HALF), f32),
            jax.ShapeDtypeStruct((TOK, HALF), f32),
            jax.ShapeDtypeStruct((TOK + OWN, HALF), f32),
        ),
        in_specs=[vmem()] * 9,
        out_specs=(vmem(), vmem(), vmem()),
        compiler_params=params(LAST_VMEM),
        name="gradients",
    )(returned, assign, *saved, w_query, w_key, w_value, w_out)
    half_shape = jax.ShapeDtypeStruct((1, TOK, HALF), bf16)
    return pl.pallas_call(
        finish_kernel,
        out_shape=(half_shape, half_shape),
        in_specs=[vmem()] * 3,
        out_specs=(vmem(), vmem()),
        compiler_params=params(LAST_VMEM),
        name="finish",
    )(attended, mine, swap_cores(other))


def solution(mesh):
    placed = (P("tm", None, None), P("tm", None), P(), P(), P(), P(), P("tm", None, None))
    return jax.shard_map(
        shards,
        mesh=mesh,
        in_specs=placed,
        out_specs=(P("tm", None, "head"), P("tm", None, "head")),
        check_vma=False,
    )
```

```python
import jax
import jax.numpy as jnp
from jax import lax
from jax.experimental import pallas as pl
from jax.experimental.pallas import tpu as pltpu
from jax.sharding import PartitionSpec as P

HEAD_DIM = 64
MEM = 32
TOK = 128
D = 1024
HALF = 512
HEADS = 16
CHIPS = 128
SPLITS = CHIPS // HEADS
OWN = TOK // 2
OWN_MEM = MEM // 2
QROWS = OWN // SPLITS
MEM_PAIRS = OWN_MEM // 2
QUERY_PAIRS = QROWS // 2
PAIRS = MEM_PAIRS + QUERY_PAIRS + 1
STATS_AT = MEM_PAIRS + QUERY_PAIRS
CHUNK_HEADS = 4
GROUP = 2
CHUNK = CHUNK_HEADS * HEAD_DIM
CHUNKS = HEADS // CHUNK_HEADS
LANES = 2 * HEAD_DIM
KEYS = CHIPS * MEM
BLOCK_SEGS = 16
QBLOCK = BLOCK_SEGS * QROWS
KBLOCK = BLOCK_SEGS * MEM
KHALF = KBLOCK // 2
NBLOCKS = CHIPS // BLOCK_SEGS
SCALE = 0.125
MASKED = -3e38
FIRST_VMEM = 60 * 1024 * 1024
MIDDLE_VMEM = 40 * 1024 * 1024
LAST_VMEM = 32 * 1024 * 1024
f32 = jnp.float32
bf16 = jnp.bfloat16


def dot(a, b):
    return jnp.dot(a, b, preferred_element_type=f32)


def dot_nt(a, b):
    return lax.dot_general(a, b, (((1,), (1,)), ((), ())), preferred_element_type=f32)


def dot_tn(a, b):
    return lax.dot_general(a, b, (((0,), (0,)), ((), ())), preferred_element_type=f32)


def three_parts(x):
    high = x.astype(bf16).astype(f32)
    rest = x - high
    middle = rest.astype(bf16).astype(f32)
    low = (rest - middle).astype(bf16).astype(f32)
    return high, middle, low


def low_lanes(shape):
    return lax.broadcasted_iota(jnp.int32, shape, 1) < HEAD_DIM


def split_pair(pair):
    low = low_lanes(pair.shape)
    zero = jnp.zeros_like(pair)
    return jnp.concatenate([jnp.where(low, pair, zero), jnp.where(low, zero, pair)], axis=0)


def head_cols(matrix, head):
    return matrix[:, head * HEAD_DIM : (head + 1) * HEAD_DIM]


def onehot_rows(assign_row, first):
    rows = lax.broadcasted_iota(jnp.int32, (OWN_MEM, TOK), 0) + first
    return (rows == assign_row).astype(f32)


def pre_kernel(
    tok_hbm, asg_hbm, cot_hbm, wq_hbm, wk_hbm, wv_hbm, wo_hbm, msg_hbm, qd_hbm, kv_hbm, side_hbm,
    tok_ref, asg_ref, cot_ref, wq, wk, wv, wo, msg_ref, qd_ref, kv_ref, side_ref, sems, w_sems, out_sems,
):
    half = lax.axis_index("head")
    own_rows = pl.ds(pl.multiple_of(half * OWN, OWN), OWN)
    moves = [(asg_hbm, asg_ref), (tok_hbm, tok_ref), (cot_hbm.at[own_rows, :], cot_ref)]
    copies = [pltpu.make_async_copy(source, target, sems.at[at]) for at, (source, target) in enumerate(moves)]
    weights = []
    for chunk in range(CHUNKS):
        cols = slice(chunk * CHUNK, (chunk + 1) * CHUNK)
        pairs = [
            (wk_hbm.at[:, cols], wk.at[:, cols]),
            (wv_hbm.at[:, cols], wv.at[:, cols]),
            (wq_hbm.at[:, cols], wq.at[:, cols]),
            (wo_hbm.at[cols, :], wo.at[cols, :]),
        ]
        weights.append(
            [pltpu.make_async_copy(source, target, w_sems.at[chunk, at]) for at, (source, target) in enumerate(pairs)]
        )
    for copy in copies + weights[0] + weights[1]:
        copy.start()
    copies[0].wait()
    onehot = onehot_rows(asg_ref[...], half * OWN_MEM)
    counts = jnp.sum(onehot, axis=1, keepdims=True)
    copies[1].wait()
    tokens = tok_ref[...]
    memory = (dot(onehot.astype(bf16), tokens) / counts).astype(bf16)
    rows = jnp.concatenate([memory, tokens], axis=0)
    own_tokens = tok_ref[own_rows, :]
    copies[2].wait()
    own_cotangent = cot_ref[...]
    lane = lax.broadcasted_iota(jnp.int32, (OWN, LANES), 1)
    sublane = lax.broadcasted_iota(jnp.int32, (OWN, LANES), 0)
    sends = []
    for chunk in range(CHUNKS):
        cols = slice(chunk * CHUNK, (chunk + 1) * CHUNK)
        for copy in weights[chunk]:
            copy.wait()
        if chunk + 2 < CHUNKS:
            for copy in weights[chunk + 2]:
                copy.start()
        keys = dot(rows, wk[:, cols]).astype(bf16)
        values = dot(rows, wv[:, cols]).astype(bf16)
        queries = (dot(own_tokens, wq[:, cols]).astype(bf16).astype(f32) * SCALE).astype(bf16)
        grad_out = dot_nt(own_cotangent, wo[cols, :]).astype(bf16)
        for at_head in range(CHUNK_HEADS):
            head = chunk * CHUNK_HEADS + at_head
            pair = jnp.concatenate([head_cols(keys, at_head), head_cols(values, at_head)], axis=1)
            query_pair = jnp.concatenate([head_cols(queries, at_head), head_cols(grad_out, at_head)], axis=1)
            kv_ref[head] = pair[OWN_MEM:]
            qd_ref[head] = query_pair
            mem_pairs = pair[:OWN_MEM].reshape(MEM_PAIRS, 2, LANES)
            msg_ref[:, head, :MEM_PAIRS] = jnp.broadcast_to(mem_pairs[None], (SPLITS, MEM_PAIRS, 2, LANES))
            msg_ref[:, head, MEM_PAIRS:STATS_AT] = query_pair.reshape(SPLITS, QUERY_PAIRS, 2, LANES)
        heads = slice(chunk * CHUNK_HEADS, (chunk + 1) * CHUNK_HEADS)
        sends.append(pltpu.make_async_copy(kv_ref.at[heads], kv_hbm.at[heads], out_sems.at[0, chunk]))
        sends.append(pltpu.make_async_copy(qd_ref.at[heads], qd_hbm.at[heads], out_sems.at[1, chunk]))
        sends[-2].start()
        sends[-1].start()
    for chunk in range(CHUNKS // GROUP):
        group = range(chunk * CHUNK_HEADS * GROUP, (chunk + 1) * CHUNK_HEADS * GROUP)
        query_pairs = [qd_ref[head] for head in group]
        low = low_lanes((OWN, LANES))
        scores = [dot_nt(jnp.where(low, q, jnp.zeros_like(q)), kv_ref[head]) for head, q in zip(group, query_pairs)]
        row_max = [jnp.max(x, axis=1, keepdims=True) for x in scores]
        raised = [jnp.exp(x - m) for x, m in zip(scores, row_max)]
        row_sum = [jnp.sum(x, axis=1, keepdims=True) for x in raised]
        sides = [dot((x / t).astype(bf16), kv_ref[head]) for head, x, t in zip(group, raised, row_sum)]
        for head, query_pair, top, total, side in zip(group, query_pairs, row_max, row_sum, sides):
            products = jnp.where(low, 0.0, query_pair.astype(f32) * side)
            delta = jnp.sum(products, axis=1, keepdims=True)
            side_ref[head] = jnp.where(lane == 0, top, jnp.where(low, total, side))
            stats = jnp.zeros((OWN, LANES), f32)
            for at, part in enumerate(three_parts(top) + three_parts(total) + three_parts(delta)):
                stats = jnp.where(lane // QROWS == at, part, stats)
            stats = jnp.where(lane % QROWS == sublane % QROWS, stats, 0.0)
            stats = jnp.sum(stats.reshape(SPLITS, QROWS, LANES), axis=1, keepdims=True)
            msg_ref[:, head, STATS_AT] = jnp.broadcast_to(stats, (SPLITS, 2, LANES)).astype(bf16)
        heads = slice(group[0], group[-1] + 1)
        sends.append(pltpu.make_async_copy(msg_ref.at[:, heads], msg_hbm.at[:, heads], out_sems.at[2, chunk]))
        sends.append(pltpu.make_async_copy(side_ref.at[heads], side_hbm.at[heads], out_sems.at[3, chunk]))
        sends[-2].start()
        sends[-1].start()
    for send in sends:
        send.wait()


def attend_kernel(
    msg_ref, away_ref, qd_hbm, own_hbm, side_hbm, tail_ref, mine_ref, other_ref, qd_ref, own_ref, side_ref,
    kv, kvt, scores, dprobs, accum, sems,
):
    moves = [(qd_hbm, qd_ref), (own_hbm, own_ref), (side_hbm, side_ref)]
    copies = [pltpu.make_async_copy(source, target, sems.at[at]) for at, (source, target) in enumerate(moves)]
    for copy in copies:
        copy.start()

    def segs(j):
        return slice(j * BLOCK_SEGS, (j + 1) * BLOCK_SEGS)

    def block(j):
        return slice(j * KBLOCK, (j + 1) * KBLOCK)

    def kv_block(j):
        return kv[block(j), :]

    eye = (
        lax.broadcasted_iota(jnp.int32, (LANES, LANES), 0) == lax.broadcasted_iota(jnp.int32, (LANES, LANES), 1)
    ).astype(bf16)
    visible = lax.broadcasted_iota(jnp.int32, (KBLOCK, QBLOCK), 0) % KHALF // OWN_MEM < (
        lax.broadcasted_iota(jnp.int32, (KBLOCK, QBLOCK), 1) // QROWS
    )

    def fold(op, x):
        return op(x.reshape(KBLOCK // 8, 8, QBLOCK), axis=0)

    row = lax.broadcasted_iota(jnp.int32, (2 * BLOCK_SEGS, QBLOCK), 0)
    column = lax.broadcasted_iota(jnp.int32, (2 * BLOCK_SEGS, QBLOCK), 1)
    spread = (row == column // QROWS * 2).astype(bf16)
    square_row = lax.broadcasted_iota(jnp.int32, (LANES, LANES), 0)
    square_column = lax.broadcasted_iota(jnp.int32, (LANES, LANES), 1)
    same_query = square_row % QROWS == square_column % QROWS
    gather = (
        lax.broadcasted_iota(jnp.int32, (16, LANES), 0) == lax.broadcasted_iota(jnp.int32, (16, LANES), 1) // QROWS
    ).astype(bf16)
    blocks = range(NBLOCKS)
    stats = [dot_tn(spread, msg_ref[segs(i), STATS_AT].reshape(2 * BLOCK_SEGS, LANES)) for i in blocks]
    stats = [dot_nt(gather, jnp.where(same_query, x, 0.0).astype(bf16)) for x in stats]
    state = [
        {
            "own_max": x[0:1] + x[1:2] + x[2:3],
            "own_sum": x[3:4] + x[4:5] + x[5:6],
            "own_delta": x[6:7] + x[7:8] + x[8:9],
        }
        for x in stats
    ]

    def score_stage(i):
        buf, mine = i % 3, state[i]
        kv[i * KBLOCK : i * KBLOCK + KHALF, :] = msg_ref[segs(i), :MEM_PAIRS].reshape(KHALF, LANES)
        kv[i * KBLOCK + KHALF : (i + 1) * KBLOCK, :] = away_ref[segs(i)].reshape(KHALF, LANES)
        kvt[:, block(i)] = dot_nt(eye, kv_block(i)).astype(bf16)
        query_pair = msg_ref[segs(i), MEM_PAIRS:STATS_AT].reshape(QBLOCK, LANES).astype(f32)
        mine["grad_t"] = query_pair.T[HEAD_DIM:]
        mine["pair_rows"] = split_pair(query_pair).astype(bf16)
        top = jnp.full((8, QBLOCK), MASKED, f32)
        for j in range(i + 1):
            both = dot_nt(kv_block(j), mine["pair_rows"])
            score = both[:, :QBLOCK]
            if j == i:
                score = jnp.where(visible, score, MASKED)
            scores[buf, block(j), :] = score
            dprobs[buf, block(j), :] = both[:, QBLOCK:]
            top = jnp.maximum(top, fold(jnp.max, score))
            yield
        mine["row_max"] = jnp.maximum(jnp.max(top, axis=0, keepdims=True), mine["own_max"])

    def middle_stage(i):
        mine = state[i] if i < NBLOCKS else None
        last = state[i - 1] if i > 0 else None
        total = jnp.zeros((8, QBLOCK), f32)
        out = jnp.zeros((LANES, QBLOCK), f32)
        grad = jnp.zeros((LANES, QBLOCK), f32)
        for j in range(min(i + 1, NBLOCKS)):
            right = []
            if mine is not None:
                raised = jnp.exp(scores[i % 3, block(j), :] - mine["row_max"])
                scores[i % 3, block(j), :] = raised
                total = total + fold(jnp.sum, raised)
                right.append(raised.astype(bf16))
            if last is not None and j < i:
                probs = scores[(i - 1) % 3, block(j), :] * last["inverse"]
                dscores = (probs * (dprobs[(i - 1) % 3, block(j), :] - last["delta"])).astype(bf16)
                both = jnp.concatenate([dscores, probs.astype(bf16)], axis=1)
                term = dot(both, last["pair_rows"])
                if j < i - 1:
                    term = accum[block(j), :] + term
                if i < NBLOCKS:
                    accum[block(j), :] = term
                else:
                    mine_ref[j * KHALF : (j + 1) * KHALF, :] = term[:KHALF]
                    other_ref[segs(j)] = term[KHALF:].astype(bf16).reshape(BLOCK_SEGS, MEM_PAIRS, 2, LANES)
                right.append(dscores)
            product = dot(kvt[:, block(j)], jnp.concatenate(right, axis=1) if len(right) > 1 else right[0])
            if mine is not None:
                out = out + product[:, :QBLOCK]
            if last is not None and j < i:
                grad = grad + product[:, -QBLOCK:]
            yield
        if mine is not None:
            own_share = mine["own_sum"] * jnp.exp(mine["own_max"] - mine["row_max"])
            row_sum = own_share + jnp.sum(total, axis=0, keepdims=True)
            inverse = 1.0 / row_sum
            out = out[HEAD_DIM:] * inverse
            mine.update(row_sum=row_sum, inverse=inverse, out=out)
            mine["delta"] = (
                jnp.sum(mine["grad_t"] * out, axis=0, keepdims=True) + own_share * inverse * mine["own_delta"]
            )
        if last is not None:
            main = jnp.concatenate([grad[:HEAD_DIM], last["out"]], axis=0).T.astype(bf16)
            tail_ref[segs(i - 1), :QUERY_PAIRS] = main.reshape(BLOCK_SEGS, QUERY_PAIRS, 2, LANES)

    for step in range(NBLOCKS + 2):
        running = []
        if step > 0:
            running.append(middle_stage(step - 1))
        if step < NBLOCKS:
            running.append(score_stage(step))
        while running:
            for one in list(running):
                if next(one, one) is one:
                    running.remove(one)

    stats = [jnp.zeros((LANES, LANES), f32) for _ in blocks]
    sent = [three_parts(one["row_max"]) + three_parts(one["row_sum"]) for one in state]
    for at in range(6):
        parts = [one[at] for one in sent]
        stats = [jnp.where(square_row // QROWS == at, part, x) for part, x in zip(parts, stats)]
    stats = [dot_nt(spread, jnp.where(same_query, x, 0.0).astype(bf16)) for x in stats]
    for i in blocks:
        tail_ref[segs(i), QUERY_PAIRS] = stats[i].astype(bf16).reshape(BLOCK_SEGS, 2, LANES)
    for copy in copies:
        copy.wait()


def join_kernel(mine_ref, other_ref, tail_ref, out_ref):
    out_ref[:, MEM_PAIRS:] = tail_ref[...]
    for j in range(NBLOCKS):
        segs = slice(j * BLOCK_SEGS, (j + 1) * BLOCK_SEGS)
        far = other_ref[segs].reshape(KHALF, LANES).astype(f32)
        total = (mine_ref[j * KHALF : (j + 1) * KHALF, :] + far).astype(bf16)
        out_ref[segs, :MEM_PAIRS] = total.reshape(BLOCK_SEGS, MEM_PAIRS, 2, LANES)


def post_kernel(
    msg_ref, asg_ref, qd_ref, kv_ref, side_ref, wq, wk, wv, wo, out_ref, mine_ref, other_ref, far,
):
    half = lax.axis_index("head")
    offset = pl.multiple_of(half * HALF, HALF)
    away = pl.multiple_of((1 - half) * HALF, HALF)
    onehot = onehot_rows(asg_ref[...], half * OWN_MEM)
    counts = jnp.sum(onehot, axis=1, keepdims=True)
    onehot = onehot.astype(bf16)
    heads = range(HEADS)
    def mem_sum(head):
        parts = [msg_ref[k, head, :MEM_PAIRS].reshape(OWN_MEM, LANES).astype(f32) for k in range(SPLITS)]
        return sum(parts[1:], parts[0])

    mem_pairs = [mem_sum(head) for head in heads]
    pair_rows = [split_pair(qd_ref[head]) for head in heads]
    both = [dot_nt(pair_rows[head], kv_ref[head]) for head in heads]
    returned = [msg_ref[:, head, MEM_PAIRS:STATS_AT].reshape(OWN, LANES).astype(f32) for head in heads]
    sublane = lax.broadcasted_iota(jnp.int32, (OWN, LANES), 0)
    lane = lax.broadcasted_iota(jnp.int32, (OWN, LANES), 1)
    same_query = sublane % QROWS == lane % QROWS

    part = lax.broadcasted_iota(jnp.int32, (LANES, 2 * LANES), 0) // QROWS
    wanted = lax.broadcasted_iota(jnp.int32, (LANES, 2 * LANES), 1) // LANES
    pick = (part // 3 == wanted).astype(bf16)

    def stats_of(head):
        stats = msg_ref[:, head, STATS_AT].astype(f32)[:, :1]
        stats = jnp.broadcast_to(stats, (SPLITS, QROWS, LANES)).reshape(OWN, LANES)
        return dot(jnp.where(same_query, stats, 0.0).astype(bf16), pick)

    stats = [stats_of(head) for head in heads]
    row_max = [x[:, :LANES] for x in stats]
    inverse = [1.0 / x[:, LANES:] for x in stats]
    shares = [
        side_ref[head][:, 1:2] * jnp.exp(side_ref[head][:, :1] - row_max[head]) * inverse[head] for head in heads
    ]
    mains = [(returned[head] + shares[head] * side_ref[head]).astype(bf16).astype(f32) for head in heads]
    products = [qd_ref[head].astype(f32) * mains[head] for head in heads]
    deltas = [jnp.sum(jnp.where(low_lanes(x.shape), 0.0, x), axis=1, keepdims=True) for x in products]
    probs = [jnp.exp(both[head][:OWN] - row_max[head]) * inverse[head] for head in heads]
    dscores = [(probs[head] * (both[head][OWN:] - deltas[head])).astype(bf16) for head in heads]
    own_grads = [dot(dscores[head], kv_ref[head]) for head in heads]
    own_pairs = [
        dot_tn(jnp.concatenate([dscores[head], probs[head].astype(bf16)], axis=0), pair_rows[head]) for head in heads
    ]
    grads = [jnp.concatenate([own_pairs[head], mem_pairs[head]], axis=0) for head in heads]
    heads_out = [x[:, HEAD_DIM:] for x in mains]
    query_grads = [((returned[head] + own_grads[head]) * SCALE)[:, :HEAD_DIM] for head in heads]
    key_grads = [x[:, :HEAD_DIM] for x in grads]
    value_grads = [x[:, HEAD_DIM:] for x in grads]

    def merge(parts):
        return jnp.concatenate(parts, axis=1).astype(bf16)

    heads_out = merge(heads_out)
    query_grads = merge(query_grads)
    key_grads = merge(key_grads)
    value_grads = merge(value_grads)
    own_rows = pl.ds(pl.multiple_of(half * OWN, OWN), OWN)
    for start, keep in ((away, False), (offset, True)):
        rows = pl.ds(start, HALF)
        total = dot_nt(key_grads, wk[rows, :]) + dot_nt(value_grads, wv[rows, :])
        high, middle, low = three_parts(total[TOK:] / counts)
        spread = dot_tn(onehot, high.astype(bf16)) + dot_tn(onehot, middle.astype(bf16)) + dot_tn(onehot, low.astype(bf16))
        if keep:
            mine_ref[...] = total[:TOK] + spread
            mine_ref[own_rows, :] += dot_nt(query_grads, wq[rows, :])
        else:
            far[...] = total[:TOK] + spread
            far[own_rows, :] += dot_nt(query_grads, wq[rows, :])
    other_ref[:TOK, :] = far[...].astype(bf16)
    other_ref[TOK:, :] = dot(heads_out, wo[:, pl.ds(away, HALF)]).astype(bf16)
    out_ref[...] = dot(heads_out, wo[:, pl.ds(offset, HALF)])


def finish_kernel(attended_ref, mine_ref, arrived_ref, out_ref, grad_ref):
    half = lax.axis_index("head")
    own_rows = pl.ds(pl.multiple_of(half * OWN, OWN), OWN)
    far_rows = pl.ds(pl.multiple_of((1 - half) * OWN, OWN), OWN)
    out_ref[0, own_rows, :] = attended_ref[...].astype(bf16)
    out_ref[0, far_rows, :] = arrived_ref[TOK:, :]
    grad_ref[0] = (mine_ref[...] + arrived_ref[:TOK, :].astype(f32)).astype(bf16)


def params(vmem_bytes):
    return pltpu.CompilerParams(vmem_limit_bytes=vmem_bytes)


def vmem():
    return pl.BlockSpec(memory_space=pltpu.VMEM)


def hbm():
    return pl.BlockSpec(memory_space=pltpu.HBM)


def anywhere():
    return pl.BlockSpec(memory_space=pl.ANY)


def swap_cores(x):
    return lax.ppermute(x, "head", [(0, 1), (1, 0)])


def shards(video, assign, w_query, w_key, w_value, w_out, cotangent):
    message_shape = (SPLITS, HEADS, PAIRS, 2, LANES)
    chip_shape = (CHIPS, PAIRS, 2, LANES)
    message, query_pairs, own_pairs, own_sides = pl.pallas_call(
        pre_kernel,
        out_shape=(
            jax.ShapeDtypeStruct(message_shape, bf16),
            jax.ShapeDtypeStruct((HEADS, OWN, LANES), bf16),
            jax.ShapeDtypeStruct((HEADS, TOK, LANES), bf16),
            jax.ShapeDtypeStruct((HEADS, OWN, LANES), f32),
        ),
        in_specs=[anywhere()] * 7,
        out_specs=(hbm(), hbm(), hbm(), hbm()),
        scratch_shapes=[
            pltpu.VMEM((TOK, D), bf16),
            pltpu.VMEM((1, TOK), jnp.int32),
            pltpu.VMEM((OWN, D), bf16),
            *[pltpu.VMEM((D, D), bf16)] * 4,
            pltpu.VMEM(message_shape, bf16),
            pltpu.VMEM((HEADS, OWN, LANES), bf16),
            pltpu.VMEM((HEADS, TOK, LANES), bf16),
            pltpu.VMEM((HEADS, OWN, LANES), f32),
            pltpu.SemaphoreType.DMA((3,)),
            pltpu.SemaphoreType.DMA((CHUNKS, 4)),
            pltpu.SemaphoreType.DMA((4, CHUNKS)),
        ],
        compiler_params=params(FIRST_VMEM),
        name="project",
    )(video[0], assign, cotangent[0], w_query, w_key, w_value, w_out)

    received = lax.all_to_all(message.reshape(chip_shape), "tm", 0, 0, tiled=True)
    away = swap_cores(received[:, :MEM_PAIRS])
    part_shape = (CHIPS, MEM_PAIRS, 2, LANES)
    tail_shape = (CHIPS, PAIRS - MEM_PAIRS, 2, LANES)
    mine_shape = (CHIPS * OWN_MEM, LANES)
    saved = (query_pairs, own_pairs, own_sides)
    tail, mine, other, *saved = pl.pallas_call(
        attend_kernel,
        out_shape=(
            jax.ShapeDtypeStruct(tail_shape, bf16),
            jax.ShapeDtypeStruct(mine_shape, f32),
            jax.ShapeDtypeStruct(part_shape, bf16),
            *[jax.ShapeDtypeStruct(one.shape, one.dtype) for one in saved],
        ),
        in_specs=[vmem(), vmem()] + [anywhere()] * 3,
        out_specs=(vmem(),) * 6,
        scratch_shapes=[
            pltpu.VMEM((KEYS, LANES), bf16),
            pltpu.VMEM((LANES, KEYS), bf16),
            pltpu.VMEM((3, KEYS, QBLOCK), f32),
            pltpu.VMEM((3, KEYS, QBLOCK), f32),
            pltpu.VMEM((KEYS, LANES), f32),
            pltpu.SemaphoreType.DMA((3,)),
        ],
        compiler_params=params(MIDDLE_VMEM),
        name="attend",
    )(received, away, *saved)
    answer = pl.pallas_call(
        join_kernel,
        out_shape=jax.ShapeDtypeStruct(chip_shape, bf16),
        in_specs=[vmem()] * 3,
        out_specs=vmem(),
        compiler_params=params(LAST_VMEM),
        name="join",
    )(mine, swap_cores(other), tail)
    returned = lax.all_to_all(answer, "tm", 0, 0, tiled=True).reshape(message_shape)

    attended, mine, other = pl.pallas_call(
        post_kernel,
        out_shape=(
            jax.ShapeDtypeStruct((OWN, HALF), f32),
            jax.ShapeDtypeStruct((TOK, HALF), f32),
            jax.ShapeDtypeStruct((TOK + OWN, HALF), bf16),
        ),
        in_specs=[vmem()] * 9,
        out_specs=(vmem(), vmem(), vmem()),
        scratch_shapes=[pltpu.VMEM((TOK, HALF), f32)],
        compiler_params=params(LAST_VMEM),
        name="gradients",
    )(returned, assign, *saved, w_query, w_key, w_value, w_out)
    half_shape = jax.ShapeDtypeStruct((1, TOK, HALF), bf16)
    return pl.pallas_call(
        finish_kernel,
        out_shape=(half_shape, half_shape),
        in_specs=[vmem()] * 3,
        out_specs=(vmem(), vmem()),
        compiler_params=params(LAST_VMEM),
        name="finish",
    )(attended, mine, swap_cores(other))


def solution(mesh):
    placed = (P("tm", None, None), P("tm", None), P(), P(), P(), P(), P("tm", None, None))
    return jax.shard_map(
        shards,
        mesh=mesh,
        in_specs=placed,
        out_specs=(P("tm", None, "head"), P("tm", None, "head")),
        check_vma=False,
    )
```
